128 devices in a mesh: tm: 16 (over y, z), batch: 8 (over x, core).
Axes of the slice: x: 4, y: 4, z: 4, core: 2. Of those that a mesh axis runs over, the one named last changes fastest.
Arguments:
- frames: bfloat16 [8, 8192, 1536], P('batch', 'tm'), may hold values from -12 to 12
- w_query: bfloat16 [1536, 768], replicated, may hold values from -0.15625 to 0.15625
- w_key: bfloat16 [1536, 768], replicated, may hold values from -0.15625 to 0.15625
- w_value: bfloat16 [1536, 768], replicated, may hold values from -0.15625 to 0.15625
- w_out: bfloat16 [768, 1536], replicated, may hold values from -0.21875 to 0.21875
- w_code: bfloat16 [1536, 18], replicated, may hold values from -0.15625 to 0.15625
- code_bias: float32 [18], replicated, may hold values from -1 to 1
- w_expand: bfloat16 [18, 1536], replicated, may hold values from -1.5 to 1.5
- w_up: bfloat16 [2048, 1536], P(('tm', 'batch')), may hold values from -0.15625 to 0.15625
- w_down: bfloat16 [2048, 1536], P(('tm', 'batch')), may hold values from -0.125 to 0.125
- decoder_stream: bfloat16 [8, 8192, 1536], P('batch', 'tm'), may hold values from -6 to 6
- cotangent: bfloat16 [8, 8192, 1536], P('batch', 'tm'), may hold values from -6 to 6
Outputs:
- grad_up: float32 [2048, 1536], P(('tm', 'batch'))
- grad_down: float32 [2048, 1536], P(('tm', 'batch'))
- frame_grad: float32 [8, 8192, 18], P('batch', 'tm')
- penalty: float32 [], replicated
The draws below stay inside these ranges and needn't reach their ends.
All inputs are finite; a program needn't handle non-finite values.
Results may differ from the reference program's by a relative error of at most 0.015.
Values may be sent and summed in bfloat16 or wider, within the bound.
A program may use at most 192 MiB of HBM per device.

```python
import math
import jax
import jax.numpy as jnp
from jax import lax

D = 1536
HEADS = 6
HD = 128
BITS = 18
FF = 2048
BLOCK = 512
RECS = 8
LENGTH = 8192


def draw_frames(key, part):
    first = jax.random.fold_in(key, 11)
    second = jax.random.fold_in(key, 12)
    third = jax.random.fold_in(key, 13)
    position = jnp.arange(LENGTH, dtype=jnp.float32) / LENGTH
    ramp = jnp.exp(jnp.log(3.0) * (position - 0.5))
    rough = jnp.exp(jax.random.uniform(second, (RECS, LENGTH, 1), minval=-1.15, maxval=1.15))
    column = jnp.exp(jax.random.uniform(third, (1, 1, D), minval=-1.15, maxval=1.15))
    base = jax.random.normal(first, (RECS, LENGTH, D))
    result = base * column * rough * ramp[None, :, None] * 0.5
    return jnp.clip(result, -12.0, 12.0).astype(jnp.bfloat16)


def level_of(rng, extent, cuts, low, top_value):
    level, own = 1.0, jax.random.fold_in(rng, 6)
    for axis_at, blocks in cuts:
        draws = jnp.exp(jax.random.uniform(jax.random.fold_in(own, axis_at), (blocks,), jnp.float32, low / len(cuts), top_value / len(cuts)))
        level = level * jnp.repeat(draws, extent[axis_at] // blocks).reshape([-1 if axis == axis_at else 1 for axis in range(len(extent))])
    return level


def noise(stream_key, shape, width, limit, split=(), kind=jnp.bfloat16):
    drawn = jax.random.normal(stream_key, shape, jnp.float32) * width
    if len(split) > 0:
        drawn = level_of(stream_key, shape, split, -0.22, 0.18) * drawn
    return jnp.clip(drawn, min=-limit, max=limit).astype(kind)


def setup_inputs(seed: int = 0) -> dict:
    key_of = jax.random.split(jax.random.key(seed), 13)
    return {
        "frames": draw_frames(jax.random.fold_in(key_of[12], 71), 0),
        "w_query": noise(key_of[1], (D, HEADS * HD), D ** -0.5, 0.15625),
        "w_key": noise(key_of[2], (D, HEADS * HD), D ** -0.5, 0.15625),
        "w_value": noise(key_of[3], (D, HEADS * HD), D ** -0.5, 0.15625),
        "w_out": noise(key_of[4], (HEADS * HD, D), (HEADS * HD) ** -0.5, 0.21875),
        "w_code": noise(key_of[5], (D, BITS), D ** -0.5, 0.15625),
        "code_bias": jnp.clip(jax.random.uniform(key_of[6], (BITS,), jnp.float32, -1.0, 1.0), -1.0, 1.0),
        "w_expand": noise(key_of[7], (BITS, D), BITS ** -0.5, 1.5),
        "w_up": noise(key_of[8], (FF, D), D ** -0.5, 0.15625, ((0, 128),)),
        "w_down": noise(key_of[9], (FF, D), FF ** -0.5, 0.125, ((0, 128),)),
        "decoder_stream": noise(key_of[10], (RECS, LENGTH, D), 1.0, 6.0, ((0, 8), (1, 16))),
        "cotangent": noise(key_of[11], (RECS, LENGTH, D), 1.0, 6.0, ((0, 8), (1, 16))),
    }


EPSILON = 1e-05
ENT_WEIGHT = 2.0
HIGH = lax.Precision.HIGHEST

def gelu_slope(values):
    coeff = math.sqrt(2.0 / math.pi)
    tangent = jnp.tanh(coeff * (values + 0.044715 * values * values * values))
    return 0.5 * (1.0 + tangent) + 0.5 * values * (1.0 - tangent * tangent) * coeff * (1.0 + 3.0 * 0.044715 * values * values)

def contract_rows(left, right):
    return lax.dot_general(left, right, (((0,), (0,)), ((), ())), preferred_element_type=jnp.float32)

def contract_cols(left, right):
    return lax.dot_general(left, right, (((1,), (1,)), ((), ())), preferred_element_type=jnp.float32)

def reference(frames, w_query, w_key, w_value, w_out, w_code, code_bias, w_expand, w_up, w_down, decoder_stream, cotangent):
    total_rows = RECS * LENGTH
    flat = frames.reshape(total_rows, D)
    scale_q = 1.0 / math.sqrt(HD)
    queries = (jnp.dot(flat, w_query, preferred_element_type=jnp.float32) * scale_q).astype(jnp.bfloat16)
    keys = jnp.dot(flat, w_key, preferred_element_type=jnp.float32).astype(jnp.bfloat16)
    values = jnp.dot(flat, w_value, preferred_element_type=jnp.float32).astype(jnp.bfloat16)
    nblocks = LENGTH // BLOCK

    def blocked(array):
        return jnp.moveaxis(array.reshape(RECS, nblocks, BLOCK, HEADS, HD), 1, 0)
    causal = jnp.arange(BLOCK)[:, None] >= jnp.arange(BLOCK)[None, :]

    def advance(history, pieces):
        query_wide = pieces[0].astype(jnp.float32)
        key_wide = pieces[1].astype(jnp.float32)
        value_wide = pieces[2].astype(jnp.float32)
        scores = jnp.einsum('rthk,rshk->rhts', query_wide, key_wide, precision=HIGH)
        scores = jnp.where(causal, scores, 0.0).astype(jnp.bfloat16)
        local = jnp.einsum('rhts,rshv->rthv', scores.astype(jnp.float32), value_wide, precision=HIGH)
        carried = jnp.einsum('rthk,rhkv->rthv', query_wide, history, precision=HIGH)
        state = jnp.einsum('rshk,rshv->rhkv', key_wide, value_wide, precision=HIGH)
        return (history + state, local + carried)
    start_state = jnp.zeros((RECS, HEADS, HD, HD), jnp.float32)
    final_state, mixed = lax.scan(advance, start_state, (blocked(queries), blocked(keys), blocked(values)))
    mixed = jnp.moveaxis(mixed, 0, 1).reshape(total_rows, HEADS, HD)
    meansq = lax.optimization_barrier(jnp.mean(mixed * mixed, axis=-1, keepdims=True))
    normed = (mixed * lax.rsqrt(meansq + EPSILON)).astype(jnp.bfloat16).reshape(total_rows, HEADS * HD)
    hidden = (flat.astype(jnp.float32) + jnp.dot(normed, w_out, preferred_element_type=jnp.float32)).astype(jnp.bfloat16)
    zvals = jnp.dot(hidden, w_code, preferred_element_type=jnp.float32) + code_bias
    smooth = jnp.tanh(zvals)
    codes = smooth.astype(jnp.bfloat16)
    stream_flat = decoder_stream.reshape(total_rows, D)
    expanded = (stream_flat.astype(jnp.float32) + jnp.dot(codes, w_expand, preferred_element_type=jnp.float32)).astype(jnp.bfloat16)
    pre = contract_cols(expanded, w_up)
    act = jax.nn.gelu(pre, approximate=True).astype(jnp.bfloat16)
    cot_flat = cotangent.reshape(total_rows, D)
    dact = contract_cols(cot_flat, w_down)
    dpre = (dact * gelu_slope(pre)).astype(jnp.bfloat16)
    grad_scale = 1.0 / math.sqrt(total_rows)
    grad_up = contract_rows(dpre, expanded) * grad_scale
    grad_down = contract_rows(act, cot_flat) * grad_scale
    dexpanded = (cot_flat.astype(jnp.float32) + jnp.dot(dpre, w_up, preferred_element_type=jnp.float32)).astype(jnp.bfloat16)
    dcodes = contract_cols(dexpanded, w_expand)
    logp = jax.nn.log_sigmoid(2.0 * zvals)
    logq = jax.nn.log_sigmoid(-2.0 * zvals)
    prob = jax.nn.sigmoid(2.0 * zvals)
    entropy = -(prob * logp + (1.0 - prob) * logq)
    pbar = lax.optimization_barrier(jnp.sum(prob, axis=0)) / total_rows
    sample = jnp.sum(entropy) / total_rows
    batch_ent = -jnp.sum(pbar * jnp.log(pbar) + (1.0 - pbar) * jnp.log(1.0 - pbar))
    penalty = sample - batch_ent
    frame_grad = dcodes * (1.0 - smooth * smooth) + ENT_WEIGHT * 2.0 * prob * (1.0 - prob) * (-2.0 * zvals - jnp.log(1.0 - pbar) + jnp.log(pbar))
    return (grad_up, grad_down, frame_grad.reshape(RECS, LENGTH, BITS), penalty)
```

```python
import math

import jax
import jax.numpy as jnp
from jax import lax
from jax.experimental import pallas as pl
from jax.experimental.pallas import tpu as pltpu
from jax.sharding import PartitionSpec as P

HEADS = 6
HD = 128
BITS = 18
PADBITS = 32
BLOCK = 512
D = 1536
INNER = HEADS * HD
UNITS = 1024
PART = 512
EPSILON = 1e-05
ENT_WEIGHT = 2.0
TOTAL = 65536
MESH = pl.DeviceIdType.MESH
BF = jnp.bfloat16
F32 = jnp.float32

ORDER = (("x", "y", "z"), ("y", "z", "x"), ("z", "x", "y"))
AXES = ("y", "z", "x")
REMOTE = 130


def nn(a, b):
    return jnp.dot(a, b, preferred_element_type=F32)


def nt(a, b):
    return lax.dot_general(a, b, (((1,), (1,)), ((), ())), preferred_element_type=F32)


def tn(a, b):
    return lax.dot_general(a, b, (((0,), (0,)), ((), ())), preferred_element_type=F32)


def fused(
    frames, wq, wk, wv, wo, wct, bias, wexp, wup, wdn, stream, cot,
    gup_out, gdn_out, fg_out, pen_out,
    fr, q_w, k_w, v_w, o_w, st, ct, up, dn, q, k, v, mix,
    own_state, a_recv, b_send, b_recv, before, hid, zt, code, dc, dc_recv,
    act, dpre, pre_t, dact_t, gd, gu, r1, s1, r2, s2, r3, ps,
    lsem, ssem, rsem,
):
    t = lax.axis_index("tm")
    b = lax.axis_index("batch")
    y, z = lax.div(t, 4), lax.rem(t, 4)
    x, c = lax.div(b, 2), lax.rem(b, 2)
    pos = {"y": y, "z": z, "x": x}

    def shifted(axis, step):
        return lax.rem(pos[axis] + step + 4, 4)

    def peer(axis, step):
        n = shifted(axis, step)
        if axis == "x":
            return (t, n * 2 + c)
        if axis == "y":
            return (n * 4 + z, b)
        return (y * 4 + n, b)

    partner = (t, x * 2 + 1 - c)
    count = [0]
    sent = []

    def send(src, dst, device):
        i = count[0]
        count[0] += 1
        copy = pltpu.make_async_remote_copy(
            src_ref=src, dst_ref=dst, send_sem=ssem.at[i], recv_sem=rsem.at[i],
            device_id=device, device_id_type=MESH,
        )
        copy.start()
        sent.append(copy)
        return copy

    loads = [0]

    def load(src, dst):
        copy = pltpu.make_async_copy(src, dst, lsem.at[loads[0]])
        loads[0] += 1
        copy.start()
        return copy

    def cols(p):
        return pl.ds(p * PART, PART)

    def at(buf, p, fixed):
        return buf.at[tuple(fixed.get(a, slice(None)) for a in AXES) + (slice(None), cols(p))]

    l_fr = load(frames, fr)
    l_k = load(wk, k_w)
    l_v = load(wv, v_w)
    l_dn = load(wdn, dn.at[y, z, x])
    l_up = load(wup, up.at[y, z, x])
    barrier = pltpu.get_barrier_semaphore()
    for axis in AXES:
        for step in (1, 2, 3):
            pl.semaphore_signal(barrier, inc=1, device_id=peer(axis, step), device_id_type=MESH)
    pl.semaphore_signal(barrier, inc=1, device_id=partner, device_id_type=MESH)
    pl.semaphore_wait(barrier, 10)

    own = {"y": y, "z": z, "x": x}
    ag1 = []
    for p in range(3):
        for step in (1, 2, 3):
            for src, buf in ((wdn, dn), (wup, up)):
                ag1.append(send(src.at[:, cols(p)], at(buf, p, own), peer(ORDER[p][0], step)))
    l_q = load(wq, q_w)
    l_o = load(wo, o_w)
    l_ct = load(cot, ct.at[pl.ds(0, BLOCK)])
    l_st = load(stream, st.at[pl.ds(0, BLOCK)])
    x_ct = send(cot, ct.at[pl.ds(BLOCK, BLOCK)], partner)
    x_st = send(stream, st.at[pl.ds(BLOCK, BLOCK)], partner)

    def project(weights, out, scale):
        def tile(i, carry):
            rows = pl.ds(pl.multiple_of(i * 256, 256), 256)
            value = nn(fr[rows, :], weights[...])
            if scale is not None:
                value = value * scale
            out[rows, :] = value.astype(BF)
            return carry

        lax.fori_loop(0, BLOCK // 256, tile, 0)

    l_fr.wait()
    l_k.wait()
    project(k_w, k, None)
    l_v.wait()
    project(v_w, v, None)

    def head_cols(h):
        return pl.ds(pl.multiple_of(h * HD, HD), HD)

    def state(h, carry):
        own_state[h] = tn(k[:, head_cols(h)], v[:, head_cols(h)]).astype(BF)
        return carry

    lax.fori_loop(0, HEADS, state, 0)
    stage_a = [send(own_state, a_recv.at[step - 1], peer("y", step)) for step in (1, 2, 3)]

    l_dn.wait()
    l_up.wait()
    for copy in ag1:
        copy.wait_recv()
    ag2 = []
    for p in range(3):
        fixed = {a: pos[a] for a in ORDER[p][1:]}
        for step in (1, 2, 3):
            for buf in (dn, up):
                ag2.append(send(at(buf, p, fixed), at(buf, p, fixed), peer(ORDER[p][1], step)))

    l_q.wait()
    project(q_w, q, 1.0 / math.sqrt(HD))

    for copy in stage_a:
        copy.wait_recv()

    def combine_a(h, carry):
        total = jnp.zeros((HD, HD), F32)
        for step in (1, 2, 3):
            total = total + jnp.where(y >= step, a_recv[step - 1, h].astype(F32), 0.0)
        before[h] = total
        b_send[0, h] = (total + own_state[h].astype(F32)).astype(BF)
        b_send[1, h] = total.astype(BF)
        return carry

    lax.fori_loop(0, HEADS, combine_a, 0)
    stage_b = [
        send(b_send.at[lax.div(z + step, 4)], b_recv.at[step - 1], peer("z", step))
        for step in (1, 2, 3)
    ]

    for copy in ag2:
        copy.wait_recv()
    ag3 = []
    for p in range(3):
        axis = ORDER[p][2]
        mine = {axis: pos[axis]}
        for buf in (dn, up):
            pair = [
                send(at(buf, p, mine), at(buf, p, mine), peer(axis, step)) for step in (1, -1)
            ]
            ag3.append(pair)

    for r in range(2):
        width = (r + 1) * 256
        keep = (
            lax.broadcasted_iota(jnp.int32, (256, width), 0) + r * 256
            >= lax.broadcasted_iota(jnp.int32, (256, width), 1)
        )

        def local(h, carry):
            hc = head_cols(h)
            s = nt(q[pl.ds(r * 256, 256), hc], k[pl.ds(0, width), hc])
            s = jnp.where(keep, s, 0.0).astype(BF)
            mix[pl.ds(r * 256, 256), hc] = nn(s, v[pl.ds(0, width), hc])
            return carry

        lax.fori_loop(0, HEADS, local, 0)

    for copy in stage_b:
        copy.wait_recv()
    l_o.wait()

    def carry_in(h, carry):
        total = before[h]
        for step in range(3):
            total = total + b_recv[step, h].astype(F32)
        history = total.astype(BF)
        hc = head_cols(h)
        m = mix[:, hc] + nn(q[:, hc], history)
        meansq = jnp.mean(m * m, axis=-1, keepdims=True)
        q[:, hc] = (m * lax.rsqrt(meansq + EPSILON)).astype(BF)
        return carry

    lax.fori_loop(0, HEADS, carry_in, 0)

    def out_tile(i, carry):
        rows = pl.ds(pl.multiple_of(i * 256, 256), 256)
        hid[rows, :] = (fr[rows, :].astype(F32) + nn(q[rows, :], o_w[...])).astype(BF)
        return carry

    lax.fori_loop(0, 2, out_tile, 0)
    zvals = nt(wct[...], hid[...]) + bias[...]
    zt[...] = zvals
    code[0] = jnp.tanh(zvals).astype(BF)
    x_code = send(code.at[0], code.at[1], partner)

    ag4 = []
    for p in range(3):
        axis = ORDER[p][2]
        pair_dn, pair_up = ag3[2 * p], ag3[2 * p + 1]
        pair_dn[0].wait_recv()
        left = {axis: shifted(axis, -1)}
        ag4.append(send(at(dn, p, left), at(dn, p, left), peer(axis, 1)))
        pair_up[1].wait_recv()
        right = {axis: shifted(axis, 1)}
        ag4.append(send(at(up, p, right), at(up, p, right), peer(axis, -1)))
        pair_dn[1].wait_recv()
        pair_up[0].wait_recv()

    def sums(slot):
        zv = zt[...]
        two = 2.0 * zv
        logp = jax.nn.log_sigmoid(two)
        logq = jax.nn.log_sigmoid(-two)
        prob = jax.nn.sigmoid(two)
        entropy = -(prob * logp + (1.0 - prob) * logq)
        row = lax.broadcasted_iota(jnp.int32, (PADBITS, 1), 0)
        probs = jnp.sum(prob, axis=1, keepdims=True)
        ents = jnp.sum(entropy, axis=1, keepdims=True)
        ent = jnp.sum(jnp.where(row < BITS, ents, 0.0), axis=0, keepdims=True)
        tile = jnp.where(row < BITS, probs, jnp.where(row == 24, ent, 0.0))
        ps[0, slot] = jnp.broadcast_to(tile, (PADBITS, 128))

    sums(c)
    p_core = send(ps.at[0, c], ps.at[0, c], partner)

    l_ct.wait()
    l_st.wait()
    x_st.wait_recv()

    def expand(slot):
        def tile(i, carry):
            tok = pl.multiple_of(i * 256, 256)
            rows = pl.ds(slot * BLOCK + tok, 256)
            grown = tn(code[slot, :, pl.ds(tok, 256)], wexp[...])
            st[rows, :] = (st[rows, :].astype(F32) + grown).astype(BF)
            return carry

        lax.fori_loop(0, 2, tile, 0)

    expand(0)
    x_code.wait_recv()
    expand(1)
    x_ct.wait_recv()

    def ps_send(stage, axis, value):
        ps[stage, pos[axis]] = value
        return [
            send(ps.at[stage, pos[axis]], ps.at[stage, pos[axis]], peer(axis, step))
            for step in (1, 2, 3)
        ]

    def ps_sum(stage):
        return ps[stage, 0] + ps[stage, 1] + ps[stage, 2] + ps[stage, 3]

    p_core.wait_recv()
    p_x = ps_send(1, "x", ps[0, 0] + ps[0, 1])

    for copy in ag4:
        copy.wait_recv()

    up_all = up.reshape(UNITS, D)
    dn_all = dn.reshape(UNITS, D)
    back = nt(wexp[...], up_all[...]).astype(BF)
    coeff = math.sqrt(2.0 / math.pi)

    def forward(i, carry):
        tok = pl.multiple_of(i * 256, 256)
        rows = pl.ds(tok, 256)
        pre_t[...] = nt(up_all[...], st[rows, :])
        dact_t[...] = nt(dn_all[...], ct[rows, :])

        def slab(j, inner):
            us = pl.ds(pl.multiple_of(j * 64, 64), 64)
            val = pre_t[us, :]
            square = val * val
            half = 0.5 * jnp.tanh(val * (square * (coeff * 0.044715) + coeff)) + 0.5
            gelu = val * half
            slope = half + gelu * (1.0 - half) * (square * (6.0 * 0.044715 * coeff) + 2.0 * coeff)
            act[us, rows] = gelu.astype(BF)
            dpre[us, rows] = (dact_t[us, :] * slope).astype(BF)
            return inner

        lax.fori_loop(0, UNITS // 64, slab, 0)
        dc[:, rows] = nn(back, dpre[:, rows])
        return carry

    lax.fori_loop(0, 4, forward, 0)
    x_dc = send(dc.at[:, pl.ds(BLOCK, BLOCK)], dc_recv, partner)

    gd_all = gd.reshape(UNITS, D)
    gu_all = gu.reshape(UNITS, D)

    def gradient(left, right, out, p):
        def tile(i, carry):
            cs = pl.ds(pl.multiple_of(p * PART + i * 256, 256), 256)
            out[:, cs] = nn(left[...], right[:, cs]).astype(BF)
            return carry

        lax.fori_loop(0, PART // 256, tile, 0)

    grads = (gd, gu)
    way = (1, -1)
    far, near, joined = {}, {}, {}

    def first_sends(m, p):
        axis = ORDER[p][2]
        s = way[m]
        far[m, p] = send(
            at(grads[m], p, {axis: shifted(axis, 2)}), r1.at[m, p, 0], peer(axis, s)
        )
        near[m, p] = send(
            at(grads[m], p, {axis: shifted(axis, -s)}), r1.at[m, p, 1], peer(axis, -s)
        )

    def forward_sum(m, p):
        axis = ORDER[p][2]
        s = way[m]
        far[m, p].wait_recv()
        block = at(grads[m], p, {axis: shifted(axis, s)})

        def add(i, carry):
            block[i] = (block[i].astype(F32) + r1[m, p, 0, i].astype(F32)).astype(BF)
            return carry

        lax.fori_loop(0, 4, add, 0)
        joined[m, p] = send(block, r1.at[m, p, 2], peer(axis, s))

    for p in range(3):
        gradient(act, ct, gd_all, p)
        first_sends(0, p)
    for p in range(3):
        gradient(dpre, st, gu_all, p)
        first_sends(1, p)
        forward_sum(0, p)

    for copy in p_x:
        copy.wait_recv()
    p_y = ps_send(2, "y", ps_sum(1))

    for p in range(3):
        forward_sum(1, p)

    second = {}
    for m in range(2):
        for p in range(3):
            axis = ORDER[p][2]
            near[m, p].wait_recv()
            joined[m, p].wait_recv()
            block = at(grads[m], p, {axis: pos[axis]})

            def total1(i, carry):
                s1[m, p, i] = (
                    block[i].astype(F32)
                    + r1[m, p, 1, i].astype(F32)
                    + r1[m, p, 2, i].astype(F32)
                ).astype(BF)
                return carry

            lax.fori_loop(0, 4, total1, 0)
            axis = ORDER[p][1]
            for step in (1, 2, 3):
                n = shifted(axis, step)
                src = s1.at[m, p, n] if p == 0 else s1.at[m, p, :, n]
                second[m, p, step] = send(src, r2.at[m, p, step - 1], peer(axis, step))

    for copy in p_y:
        copy.wait_recv()
    p_z = ps_send(3, "z", ps_sum(2))

    third = {}
    for m in range(2):
        for p in range(3):
            axis = ORDER[p][1]
            for step in (1, 2, 3):
                second[m, p, step].wait_recv()
            mine = s1.at[m, p, pos[axis]] if p == 0 else s1.at[m, p, :, pos[axis]]
            total = mine[...].astype(F32)
            for step in range(3):
                total = total + r2[m, p, step].astype(F32)
            s2[m, p] = total.astype(BF)
            axis = ORDER[p][0]
            for step in (1, 2, 3):
                third[m, p, step] = send(
                    s2.at[m, p, shifted(axis, step)], r3.at[m, p, step - 1], peer(axis, step)
                )

    for copy in p_z:
        copy.wait_recv()
    x_dc.wait_recv()
    sums_all = ps_sum(3)
    row = lax.broadcasted_iota(jnp.int32, (PADBITS, 128), 0)
    pbar = jnp.where(row < BITS, sums_all / TOTAL, 0.5)
    lp, lq = jnp.log(pbar), jnp.log(1.0 - pbar)
    spread = jnp.where(row < BITS, -(pbar * lp + (1.0 - pbar) * lq), 0.0)
    batch_ent = jnp.sum(spread, axis=0, keepdims=True)
    pen_out[...] = jnp.broadcast_to(sums_all[24:25, :] / TOTAL - batch_ent, (8, 128))
    zv = zt[...]
    smooth = jnp.tanh(zv)
    prob = jax.nn.sigmoid(2.0 * zv)
    dcodes = nt(wexp[...], ct[pl.ds(0, BLOCK), :]) + dc[:, pl.ds(0, BLOCK)] + dc_recv[...]
    fg_out[...] = dcodes * (1.0 - smooth * smooth) + ENT_WEIGHT * 2.0 * prob * (1.0 - prob) * (
        -2.0 * zv - lq[:, :1] + lp[:, :1]
    )

    scale = 1.0 / math.sqrt(TOTAL)
    for m, out in ((0, gdn_out), (1, gup_out)):
        for p in range(3):
            axis = ORDER[p][0]
            total = s2[m, p, pos[axis]].astype(F32)
            for step in (1, 2, 3):
                third[m, p, step].wait_recv()
                total = total + r3[m, p, step - 1].astype(F32)
            out[:, cols(p)] = total * scale
    for copy in sent:
        copy.wait_send()


def body(
    frames, w_query, w_key, w_value, w_out, w_code, code_bias, w_expand, w_up, w_down,
    decoder_stream, cotangent,
):
    spare = PADBITS - BITS
    wct = jnp.pad(w_code.T, ((0, spare), (0, 0)))
    wexp = jnp.pad(w_expand, ((0, spare), (0, 0)))
    bias = jnp.pad(code_bias, (0, spare)).reshape(PADBITS, 1)
    anywhere = pl.BlockSpec(memory_space=pl.ANY)
    vmem = pl.BlockSpec(memory_space=pltpu.VMEM)
    state = (HEADS, HD, HD)
    scratch = [
        pltpu.VMEM((BLOCK, D), BF),
        pltpu.VMEM((D, INNER), BF),
        pltpu.VMEM((D, INNER), BF),
        pltpu.VMEM((D, INNER), BF),
        pltpu.VMEM((INNER, D), BF),
        pltpu.VMEM((2 * BLOCK, D), BF),
        pltpu.VMEM((2 * BLOCK, D), BF),
        pltpu.VMEM((4, 4, 4, 16, D), BF),
        pltpu.VMEM((4, 4, 4, 16, D), BF),
        pltpu.VMEM((BLOCK, INNER), BF),
        pltpu.VMEM((BLOCK, INNER), BF),
        pltpu.VMEM((BLOCK, INNER), BF),
        pltpu.VMEM((BLOCK, INNER), F32),
        pltpu.VMEM(state, BF),
        pltpu.VMEM((3,) + state, BF),
        pltpu.VMEM((2,) + state, BF),
        pltpu.VMEM((3,) + state, BF),
        pltpu.VMEM(state, F32),
        pltpu.VMEM((BLOCK, D), BF),
        pltpu.VMEM((PADBITS, BLOCK), F32),
        pltpu.VMEM((2, PADBITS, BLOCK), BF),
        pltpu.VMEM((PADBITS, 2 * BLOCK), F32),
        pltpu.VMEM((PADBITS, BLOCK), F32),
        pltpu.VMEM((UNITS, 2 * BLOCK), BF),
        pltpu.VMEM((UNITS, 2 * BLOCK), BF),
        pltpu.VMEM((UNITS, 256), F32),
        pltpu.VMEM((UNITS, 256), F32),
        pltpu.VMEM((4, 4, 4, 16, D), BF),
        pltpu.VMEM((4, 4, 4, 16, D), BF),
        pltpu.VMEM((2, 3, 3, 4, 4, 16, PART), BF),
        pltpu.VMEM((2, 3, 4, 4, 16, PART), BF),
        pltpu.VMEM((2, 3, 3, 4, 16, PART), BF),
        pltpu.VMEM((2, 3, 4, 16, PART), BF),
        pltpu.VMEM((2, 3, 3, 16, PART), BF),
        pltpu.VMEM((4, 4, PADBITS, 128), F32),
        pltpu.SemaphoreType.DMA((16,)),
        pltpu.SemaphoreType.DMA((REMOTE,)),
        pltpu.SemaphoreType.DMA((REMOTE,)),
    ]
    grad_up, grad_down, fg, pen = pl.pallas_call(
        fused,
        out_shape=(
            jax.ShapeDtypeStruct((16, D), F32),
            jax.ShapeDtypeStruct((16, D), F32),
            jax.ShapeDtypeStruct((PADBITS, BLOCK), F32),
            jax.ShapeDtypeStruct((8, 128), F32),
        ),
        in_specs=[anywhere] * 5 + [vmem] * 3 + [anywhere] * 4,
        out_specs=(vmem,) * 4,
        scratch_shapes=scratch,
        compiler_params=pltpu.CompilerParams(
            collective_id=0, has_side_effects=True, vmem_limit_bytes=60 * 1024 * 1024
        ),
    )(
        frames.reshape(BLOCK, D), w_query, w_key, w_value, w_out, wct, bias, wexp,
        w_up, w_down, decoder_stream.reshape(BLOCK, D), cotangent.reshape(BLOCK, D),
    )
    return grad_up, grad_down, fg[:BITS].T.reshape(1, BLOCK, BITS), pen[0, 0]


def solution(mesh):
    in_specs = (
        P("batch", "tm", None),
        P(),
        P(),
        P(),
        P(),
        P(),
        P(),
        P(),
        P(("tm", "batch"), None),
        P(("tm", "batch"), None),
        P("batch", "tm", None),
        P("batch", "tm", None),
    )
    out_specs = (P(("tm", "batch"), None), P(("tm", "batch"), None), P("batch", "tm", None), P())
    return jax.shard_map(body, mesh=mesh, in_specs=in_specs, out_specs=out_specs, check_vma=False)
```

```python
import math

import jax
import jax.numpy as jnp
from jax import lax
from jax.experimental import pallas as pl
from jax.experimental.pallas import tpu as pltpu
from jax.sharding import PartitionSpec as P

HEADS = 6
HD = 128
BITS = 18
PADBITS = 32
BLOCK = 512
D = 1536
INNER = HEADS * HD
UNITS = 1024
PART = 512
EPSILON = 1e-05
ENT_WEIGHT = 2.0
TOTAL = 65536
MESH = pl.DeviceIdType.MESH
BF = jnp.bfloat16
F32 = jnp.float32

ORDER = (("x", "y", "z"), ("y", "z", "x"), ("z", "x", "y"))
AXES = ("y", "z", "x")
REMOTE = 188
SHARE = INNER // 16


def nn(a, b):
    return jnp.dot(a, b, preferred_element_type=F32)


def nt(a, b):
    return lax.dot_general(a, b, (((1,), (1,)), ((), ())), preferred_element_type=F32)


def tn(a, b):
    return lax.dot_general(a, b, (((0,), (0,)), ((), ())), preferred_element_type=F32)


def fused(
    frames, wq, wk, wv, wo, wct, bias, wexp, wup, wdn, stream, cot,
    gup_out, gdn_out, fg_out, pen_out,
    fr, q_w, k_w, v_w, o_w, st, ct, up, dn, q, k, v, mix,
    own_state, a_recv, prefix, history, hid, zt, code, dc, dc_recv,
    act, dpre, pre_a, pre_b, slope, gd, gu, r1, s1, r2, s2, r3, ps,
    lsem, ssem, rsem,
):
    t = lax.axis_index("tm")
    b = lax.axis_index("batch")
    y, z = lax.div(t, 4), lax.rem(t, 4)
    x, c = lax.div(b, 2), lax.rem(b, 2)
    pos = {"y": y, "z": z, "x": x}

    def shifted(axis, step):
        return lax.rem(pos[axis] + step + 4, 4)

    def peer(axis, step):
        n = shifted(axis, step)
        if axis == "x":
            return (t, n * 2 + c)
        if axis == "y":
            return (n * 4 + z, b)
        return (y * 4 + n, b)

    partner = (t, x * 2 + 1 - c)
    count = [0]
    sent = []

    def send(src, dst, device):
        i = count[0]
        count[0] += 1
        copy = pltpu.make_async_remote_copy(
            src_ref=src, dst_ref=dst, send_sem=ssem.at[i], recv_sem=rsem.at[i],
            device_id=device, device_id_type=MESH,
        )
        copy.start()
        sent.append(copy)
        return copy

    loads = [0]

    def load(src, dst):
        copy = pltpu.make_async_copy(src, dst, lsem.at[loads[0]])
        loads[0] += 1
        copy.start()
        return copy

    def cols(p):
        return pl.ds(p * PART, PART)

    def at(buf, p, fixed):
        return buf.at[tuple(fixed.get(a, slice(None)) for a in AXES) + (slice(None), cols(p))]

    barrier = pltpu.get_barrier_semaphore()
    others = [(lax.rem(t + j, 16), b) for j in range(1, 16)]
    for device in others + [peer("x", 1), peer("x", 2), peer("x", 3), partner]:
        pl.semaphore_signal(barrier, inc=1, device_id=device, device_id_type=MESH)
    l_fr = load(frames, fr)
    l_k = load(wk, k_w)
    l_v = load(wv, v_w)
    l_dn = load(wdn, dn.at[y, z, x])
    l_up = load(wup, up.at[y, z, x])
    l_q = load(wq, q_w)
    pl.semaphore_wait(barrier, 19)

    shards = {"up": (wup, up), "dn": (wdn, dn)}
    ag1, ag2, ag3, ag4 = {}, {}, {}, {}

    def half(buf, p, axis, n, h):
        fixed = {a: slice(None) for a in AXES}
        fixed[axis] = n
        fixed[ORDER[p][0]] = pl.ds(2 * h, 2)
        return at(buf, p, fixed)

    for m in ("up", "dn"):
        src, buf = shards[m]
        for p in range(3):
            ag1[m, p] = [
                send(src.at[:, cols(p)], at(buf, p, pos), peer(ORDER[p][0], step))
                for step in (2, 1, 3)
            ]

    def gather_second(m):
        buf = shards[m][1]
        for p in range(3):
            for copy in ag1[m, p]:
                copy.wait_recv()
            fixed = {a: pos[a] for a in ORDER[p][1:]}
            ag2[m, p] = [
                send(at(buf, p, fixed), at(buf, p, fixed), peer(ORDER[p][1], step))
                for step in (2, 1, 3)
            ]

    def gather_third(m, first):
        buf = shards[m][1]
        for p in range(3):
            axis = ORDER[p][2]
            if first:
                for copy in ag2[m, p]:
                    copy.wait_recv()
            for step in (1, -1):
                h = int((step == 1) != first)
                mine = half(buf, p, axis, pos[axis], h)
                ag3[m, p, step, first] = send(mine, mine, peer(axis, step))

    def gather_last(m):
        buf = shards[m][1]
        for p in range(3):
            axis = ORDER[p][2]
            for step in (1, -1):
                ag3[m, p, step, True].wait_recv()
                block = half(buf, p, axis, shifted(axis, -step), int(step == -1))
                ag4[m, p, step] = send(block, block, peer(axis, step))

    def gather_end(m):
        for p in range(3):
            for step in (1, -1):
                ag3[m, p, step, False].wait_recv()
                ag4[m, p, step].wait_recv()

    l_o = load(wo, o_w)
    l_ct = load(cot, ct.at[pl.ds(0, BLOCK)])
    l_st = load(stream, st.at[pl.ds(0, BLOCK)])
    x_ct = send(cot, ct.at[pl.ds(BLOCK, BLOCK)], partner)
    x_st = send(stream, st.at[pl.ds(BLOCK, BLOCK)], partner)

    def project(weights, out, scale):
        def tile(i, carry):
            rows = pl.ds(pl.multiple_of(i * 256, 256), 256)
            value = nn(fr[rows, :], weights[...])
            if scale is not None:
                value = value * scale
            out[rows, :] = value.astype(BF)
            return carry

        lax.fori_loop(0, BLOCK // 256, tile, 0)

    l_fr.wait()
    l_k.wait()
    project(k_w, k, None)
    l_dn.wait()
    l_up.wait()
    gather_second("up")
    l_v.wait()
    project(v_w, v, None)

    def head_cols(h):
        return pl.ds(pl.multiple_of(h * HD, HD), HD)

    def state(h, carry):
        rows = pl.ds(pl.multiple_of(h * HD, HD), HD)
        own_state[rows, :] = tn(k[:, head_cols(h)], v[:, head_cols(h)]).astype(BF)
        return carry

    lax.fori_loop(0, HEADS, state, 0)

    def share(n):
        return pl.ds(pl.multiple_of(n * SHARE, SHARE), SHARE)

    to_share = [send(own_state.at[share(d[0])], a_recv.at[t], d) for d in others]
    a_recv[t] = own_state[share(t), :]
    gather_second("dn")
    l_q.wait()
    project(q_w, q, 1.0 / math.sqrt(HD))
    def local_rows(r):
        width = (r + 1) * 256
        keep = (
            lax.broadcasted_iota(jnp.int32, (256, width), 0) + r * 256
            >= lax.broadcasted_iota(jnp.int32, (256, width), 1)
        )

        def local(h, carry):
            hc = head_cols(h)
            s = nt(q[pl.ds(r * 256, 256), hc], k[pl.ds(0, width), hc])
            s = jnp.where(keep, s, 0.0).astype(BF)
            mix[pl.ds(r * 256, 256), hc] = nn(s, v[pl.ds(0, width), hc])
            return carry

        lax.fori_loop(0, HEADS, local, 0)

    local_rows(0)
    for copy in to_share:
        copy.wait_recv()
    running = jnp.zeros((SHARE, HD), F32)
    for n in range(16):
        prefix[n] = running.astype(BF)
        if n < 15:
            running = running + a_recv[n].astype(F32)
    from_share = [send(prefix.at[d[0]], history.at[share(t)], d) for d in others]
    history[share(t), :] = prefix[t]

    gather_third("up", True)
    gather_third("up", False)
    local_rows(1)
    gather_third("dn", True)

    for copy in from_share:
        copy.wait_recv()
    l_o.wait()

    def carry_in(h, carry):
        hc = head_cols(h)
        m = mix[:, hc] + nn(q[:, hc], history[hc, :])
        meansq = jnp.mean(m * m, axis=-1, keepdims=True)
        q[:, hc] = (m * lax.rsqrt(meansq + EPSILON)).astype(BF)
        return carry

    lax.fori_loop(0, HEADS, carry_in, 0)

    def out_tile(i, carry):
        rows = pl.ds(pl.multiple_of(i * 256, 256), 256)
        hid[rows, :] = (fr[rows, :].astype(F32) + nn(q[rows, :], o_w[...])).astype(BF)
        return carry

    lax.fori_loop(0, 2, out_tile, 0)
    zvals = nt(wct[...], hid[...]) + bias[...]
    zt[...] = zvals
    code[0] = jnp.tanh(zvals).astype(BF)
    x_code = send(code.at[0], code.at[1], partner)

    gather_last("up")
    gather_third("dn", False)

    def sums(slot):
        zv = zt[...]
        two = 2.0 * zv
        logp = jax.nn.log_sigmoid(two)
        logq = jax.nn.log_sigmoid(-two)
        prob = jax.nn.sigmoid(two)
        entropy = -(prob * logp + (1.0 - prob) * logq)
        row = lax.broadcasted_iota(jnp.int32, (PADBITS, 1), 0)
        probs = jnp.sum(prob, axis=1, keepdims=True)
        ents = jnp.sum(entropy, axis=1, keepdims=True)
        ent = jnp.sum(jnp.where(row < BITS, ents, 0.0), axis=0, keepdims=True)
        tile = jnp.where(row < BITS, probs, jnp.where(row == 24, ent, 0.0))
        ps[0, slot] = jnp.broadcast_to(tile, (PADBITS, 128))

    sums(c)
    p_core = send(ps.at[0, c], ps.at[0, c], partner)

    l_ct.wait()
    l_st.wait()
    x_st.wait_recv()

    def expand(slot):
        def tile(i, carry):
            tok = pl.multiple_of(i * 256, 256)
            rows = pl.ds(slot * BLOCK + tok, 256)
            grown = tn(code[slot, :, pl.ds(tok, 256)], wexp[...])
            st[rows, :] = (st[rows, :].astype(F32) + grown).astype(BF)
            return carry

        lax.fori_loop(0, 2, tile, 0)

    expand(0)
    x_code.wait_recv()
    expand(1)
    gather_last("dn")

    def ps_send(stage, axis, value):
        ps[stage, pos[axis]] = value
        return [
            send(ps.at[stage, pos[axis]], ps.at[stage, pos[axis]], peer(axis, step))
            for step in (1, 2, 3)
        ]

    def ps_sum(stage):
        return ps[stage, 0] + ps[stage, 1] + ps[stage, 2] + ps[stage, 3]

    p_core.wait_recv()
    p_x = ps_send(1, "x", ps[0, 0] + ps[0, 1])

    gather_end("up")

    up_all = up.reshape(UNITS, D)
    dn_all = dn.reshape(UNITS, D)
    tiles = [pl.ds(i * 256, 256) for i in range(4)]
    coeff = math.sqrt(2.0 / math.pi)
    buffers = (pre_a, pre_b)

    def act_slabs(rows, pre):
        for j in range(UNITS // 64):
            us = pl.ds(j * 64, 64)
            val = pre[us, :]
            square = val * val
            half_t = 0.5 * jnp.tanh(val * (square * (coeff * 0.044715) + coeff)) + 0.5
            gelu = val * half_t
            act[us, rows] = gelu.astype(BF)
            slope[us, rows] = half_t + gelu * (1.0 - half_t) * (
                square * (6.0 * 0.044715 * coeff) + 2.0 * coeff
            )

    for i in range(5):
        if i < 4:
            buffers[i % 2][...] = nt(up_all[...], st[tiles[i], :])
        if i > 0:
            act_slabs(tiles[i - 1], buffers[(i - 1) % 2])

    def dpre_all():
        for i in range(5):
            if i < 4:
                buffers[i % 2][...] = nt(dn_all[...], ct[tiles[i], :])
            if i > 0:
                for j in range(UNITS // 64):
                    us = pl.ds(j * 64, 64)
                    dpre[us, tiles[i - 1]] = (
                        buffers[(i - 1) % 2][us, :] * slope[us, tiles[i - 1]]
                    ).astype(BF)

    gd_all = gd.reshape(UNITS, D)
    gu_all = gu.reshape(UNITS, D)

    def gradient(left, right, out, p):
        def tile(i, carry):
            cs = pl.ds(pl.multiple_of(p * PART + i * 256, 256), 256)
            out[:, cs] = nn(left[...], right[:, cs]).astype(BF)
            return carry

        lax.fori_loop(0, PART // 256, tile, 0)

    grads = (gd, gu)
    far, plain, joined, second, third = {}, {}, {}, {}, {}

    def landing(m, p, slot, h):
        if p == 0:
            return r1.at[m, p, slot, :, pl.ds(2 * h, 2)]
        return r1.at[m, p, slot, pl.ds(2 * h, 2)] if p == 1 else r1.at[m, p, slot, pl.ds(2 * h, 2)]

    def first_sends(m, p):
        axis = ORDER[p][2]
        for step in (1, -1):
            h = int(step == -1)
            far[m, p, step] = send(
                half(grads[m], p, axis, shifted(axis, 2), h), landing(m, p, 0, h), peer(axis, step)
            )
        for step in (1, -1):
            h = int(step == 1)
            slot = 1 if step == 1 else 2
            plain[m, p, step] = send(
                half(grads[m], p, axis, shifted(axis, step), h),
                landing(m, p, slot, h),
                peer(axis, step),
            )

    def forward_sum(m, p):
        axis = ORDER[p][2]
        for step in (1, -1):
            h = int(step == -1)
            slot = 1 if step == 1 else 2
            far[m, p, step].wait_recv()
            block = half(grads[m], p, axis, shifted(axis, step), h)
            came = landing(m, p, 0, h)
            block[...] = (block[...].astype(F32) + came[...].astype(F32)).astype(BF)
            joined[m, p, step] = send(block, landing(m, p, slot, h), peer(axis, step))

    def second_sends(m, p):
        axis = ORDER[p][2]
        for step in (1, -1):
            plain[m, p, step].wait_recv()
            joined[m, p, step].wait_recv()
        block = at(grads[m], p, {axis: pos[axis]})

        def total1(i, carry):
            s1[m, p, i] = (
                block[i].astype(F32)
                + r1[m, p, 1, i].astype(F32)
                + r1[m, p, 2, i].astype(F32)
            ).astype(BF)
            return carry

        lax.fori_loop(0, 4, total1, 0)
        axis = ORDER[p][1]
        for step in (2, 1, 3):
            n = shifted(axis, step)
            src = s1.at[m, p, n] if p == 0 else s1.at[m, p, :, n]
            second[m, p, step] = send(src, r2.at[m, p, step - 1], peer(axis, step))

    def third_sends(m, p):
        axis = ORDER[p][1]
        for step in (1, 2, 3):
            second[m, p, step].wait_recv()
        mine = s1.at[m, p, pos[axis]] if p == 0 else s1.at[m, p, :, pos[axis]]
        total = mine[...].astype(F32)
        for step in range(3):
            total = total + r2[m, p, step].astype(F32)
        s2[m, p] = total.astype(BF)
        axis = ORDER[p][0]
        for step in (2, 1, 3):
            third[m, p, step] = send(
                s2.at[m, p, shifted(axis, step)], r3.at[m, p, step - 1], peer(axis, step)
            )

    scale = 1.0 / math.sqrt(TOTAL)

    def last_sum(m, p):
        out = (gdn_out, gup_out)[m]
        axis = ORDER[p][0]
        total = s2[m, p, pos[axis]].astype(F32)
        for step in (1, 2, 3):
            third[m, p, step].wait_recv()
            total = total + r3[m, p, step - 1].astype(F32)
        out[:, cols(p)] = total * scale

    x_ct.wait_recv()
    for p in range(3):
        gradient(act, ct, gd_all, p)
        first_sends(0, p)
    gather_end("dn")
    dpre_all()
    for p in range(3):
        forward_sum(0, p)
    for p in range(3):
        gradient(dpre, st, gu_all, p)
        first_sends(1, p)
    for copy in p_x:
        copy.wait_recv()
    p_y = ps_send(2, "y", ps_sum(1))
    back = nt(wexp[...], up_all[...]).astype(BF)

    for i in range(4):
        dc[:, tiles[i]] = nn(back, dpre[:, tiles[i]])
    x_dc = send(dc.at[:, pl.ds(BLOCK, BLOCK)], dc_recv, partner)
    for copy in p_y:
        copy.wait_recv()
    p_z = ps_send(3, "z", ps_sum(2))

    for p in range(3):
        second_sends(0, p)
    for p in range(3):
        forward_sum(1, p)
    for p in range(3):
        third_sends(0, p)
    for p in range(3):
        second_sends(1, p)

    for copy in p_z:
        copy.wait_recv()
    x_dc.wait_recv()
    sums_all = ps_sum(3)
    row = lax.broadcasted_iota(jnp.int32, (PADBITS, 128), 0)
    pbar = jnp.where(row < BITS, sums_all / TOTAL, 0.5)
    lp, lq = jnp.log(pbar), jnp.log(1.0 - pbar)
    spread = jnp.where(row < BITS, -(pbar * lp + (1.0 - pbar) * lq), 0.0)
    batch_ent = jnp.sum(spread, axis=0, keepdims=True)
    pen_out[...] = jnp.broadcast_to(sums_all[24:25, :] / TOTAL - batch_ent, (8, 128))
    zv = zt[...]
    smooth = jnp.tanh(zv)
    prob = jax.nn.sigmoid(2.0 * zv)
    dcodes = nt(wexp[...], ct[pl.ds(0, BLOCK), :]) + dc[:, pl.ds(0, BLOCK)] + dc_recv[...]
    fg_out[...] = dcodes * (1.0 - smooth * smooth) + ENT_WEIGHT * 2.0 * prob * (1.0 - prob) * (
        -2.0 * zv - lq[:, :1] + lp[:, :1]
    )

    for p in range(3):
        last_sum(0, p)
    for p in range(3):
        third_sends(1, p)
    for p in range(3):
        last_sum(1, p)
    for copy in sent:
        copy.wait_send()


def body(
    frames, w_query, w_key, w_value, w_out, w_code, code_bias, w_expand, w_up, w_down,
    decoder_stream, cotangent,
):
    spare = PADBITS - BITS
    wct = jnp.pad(w_code.T, ((0, spare), (0, 0)))
    wexp = jnp.pad(w_expand, ((0, spare), (0, 0)))
    bias = jnp.pad(code_bias, (0, spare)).reshape(PADBITS, 1)
    anywhere = pl.BlockSpec(memory_space=pl.ANY)
    vmem = pl.BlockSpec(memory_space=pltpu.VMEM)
    scratch = [
        pltpu.VMEM((BLOCK, D), BF),
        pltpu.VMEM((D, INNER), BF),
        pltpu.VMEM((D, INNER), BF),
        pltpu.VMEM((D, INNER), BF),
        pltpu.VMEM((INNER, D), BF),
        pltpu.VMEM((2 * BLOCK, D), BF),
        pltpu.VMEM((2 * BLOCK, D), BF),
        pltpu.VMEM((4, 4, 4, 16, D), BF),
        pltpu.VMEM((4, 4, 4, 16, D), BF),
        pltpu.VMEM((BLOCK, INNER), BF),
        pltpu.VMEM((BLOCK, INNER), BF),
        pltpu.VMEM((BLOCK, INNER), BF),
        pltpu.VMEM((BLOCK, INNER), F32),
        pltpu.VMEM((INNER, HD), BF),
        pltpu.VMEM((16, SHARE, HD), BF),
        pltpu.VMEM((16, SHARE, HD), BF),
        pltpu.VMEM((INNER, HD), BF),
        pltpu.VMEM((BLOCK, D), BF),
        pltpu.VMEM((PADBITS, BLOCK), F32),
        pltpu.VMEM((2, PADBITS, BLOCK), BF),
        pltpu.VMEM((PADBITS, 2 * BLOCK), F32),
        pltpu.VMEM((PADBITS, BLOCK), F32),
        pltpu.VMEM((UNITS, 2 * BLOCK), BF),
        pltpu.VMEM((UNITS, 2 * BLOCK), BF),
        pltpu.VMEM((UNITS, 256), F32),
        pltpu.VMEM((UNITS, 256), F32),
        pltpu.VMEM((UNITS, 2 * BLOCK), F32),
        pltpu.VMEM((4, 4, 4, 16, D), BF),
        pltpu.VMEM((4, 4, 4, 16, D), BF),
        pltpu.VMEM((2, 3, 3, 4, 4, 16, PART), BF),
        pltpu.VMEM((2, 3, 4, 4, 16, PART), BF),
        pltpu.VMEM((2, 3, 3, 4, 16, PART), BF),
        pltpu.VMEM((2, 3, 4, 16, PART), BF),
        pltpu.VMEM((2, 3, 3, 16, PART), BF),
        pltpu.VMEM((4, 4, PADBITS, 128), F32),
        pltpu.SemaphoreType.DMA((16,)),
        pltpu.SemaphoreType.DMA((REMOTE,)),
        pltpu.SemaphoreType.DMA((REMOTE,)),
    ]
    grad_up, grad_down, fg, pen = pl.pallas_call(
        fused,
        out_shape=(
            jax.ShapeDtypeStruct((16, D), F32),
            jax.ShapeDtypeStruct((16, D), F32),
            jax.ShapeDtypeStruct((PADBITS, BLOCK), F32),
            jax.ShapeDtypeStruct((8, 128), F32),
        ),
        in_specs=[anywhere] * 5 + [vmem] * 3 + [anywhere] * 4,
        out_specs=(vmem,) * 4,
        scratch_shapes=scratch,
        compiler_params=pltpu.CompilerParams(
            collective_id=0, has_side_effects=True, vmem_limit_bytes=60 * 1024 * 1024
        ),
    )(
        frames.reshape(BLOCK, D), w_query, w_key, w_value, w_out, wct, bias, wexp,
        w_up, w_down, decoder_stream.reshape(BLOCK, D), cotangent.reshape(BLOCK, D),
    )
    return grad_up, grad_down, fg[:BITS].T.reshape(1, BLOCK, BITS), pen[0, 0]


def solution(mesh):
    in_specs = (
        P("batch", "tm", None),
        P(),
        P(),
        P(),
        P(),
        P(),
        P(),
        P(),
        P(("tm", "batch"), None),
        P(("tm", "batch"), None),
        P("batch", "tm", None),
        P("batch", "tm", None),
    )
    out_specs = (P(("tm", "batch"), None), P(("tm", "batch"), None), P("batch", "tm", None), P())
    return jax.shard_map(body, mesh=mesh, in_specs=in_specs, out_specs=out_specs, check_vma=False)
```

```python
import math

import jax
import jax.numpy as jnp
from jax import lax
from jax.experimental import pallas as pl
from jax.experimental.pallas import tpu as pltpu
from jax.sharding import PartitionSpec as P

HEADS = 6
HD = 128
BITS = 18
PADBITS = 32
BLOCK = 512
D = 1536
INNER = HEADS * HD
UNITS = 1024
PART = 512
EPSILON = 1e-05
ENT_WEIGHT = 2.0
TOTAL = 65536
MESH = pl.DeviceIdType.MESH
BF = jnp.bfloat16
F32 = jnp.float32

ORDER = (("x", "y", "z"), ("y", "z", "x"), ("z", "x", "y"))
AXES = ("y", "z", "x")
ARRIVALS = 58
DEPARTURES = 17
SHARE = INNER // 16


def nn(a, b):
    return jnp.dot(a, b, preferred_element_type=F32)


def nt(a, b):
    return lax.dot_general(a, b, (((1,), (1,)), ((), ())), preferred_element_type=F32)


def tn(a, b):
    return lax.dot_general(a, b, (((0,), (0,)), ((), ())), preferred_element_type=F32)


def fused(
    frames, wq, wk, wv, wo, w_code, bias, w_exp, wup, wdn, stream, cot,
    grad_out, fg_out, pen_out,
    fr, q_w, k_w, v_w, o_w, st, ct, up, dn, q, k, v, mix,
    own_state, a_recv, prefix, history, hid, zt, code, dc, dc_recv,
    wexp, act, dpre, pre_a, pre_b, slope, gd, gu, r1, s1, r2, s2, r3, ps,
    lsem, ssem, rsem,
):
    t = lax.axis_index("tm")
    b = lax.axis_index("batch")
    y, z = lax.div(t, 4), lax.rem(t, 4)
    x, c = lax.div(b, 2), lax.rem(b, 2)
    pos = {"y": y, "z": z, "x": x}

    def shifted(axis, step):
        return lax.rem(pos[axis] + step + 4, 4)

    def peer(axis, step):
        n = shifted(axis, step)
        if axis == "x":
            return (t, n * 2 + c)
        if axis == "y":
            return (n * 4 + z, b)
        return (y * 4 + n, b)

    partner = (t, x * 2 + 1 - c)
    arrivals, departures = {}, {}

    def semaphores(arrival, departure):
        return (
            ssem.at[departures.setdefault(departure, len(departures))],
            rsem.at[arrivals.setdefault(arrival, len(arrivals))],
        )

    def send(src, dst, device, arrival, departure):
        out, into = semaphores(arrival, departure)
        pltpu.make_async_remote_copy(
            src_ref=src, dst_ref=dst, send_sem=out, recv_sem=into,
            device_id=device, device_id_type=MESH,
        ).start()

    def waiter(arrival, departure, size):
        out, into = semaphores(arrival, departure)
        return pltpu.make_async_remote_copy(
            src_ref=size, dst_ref=size, send_sem=out, recv_sem=into,
            device_id=partner, device_id_type=MESH,
        )

    def arrived(arrival, size):
        waiter(arrival, "ag1", size).wait_recv()

    def departed(departure, size):
        waiter("a1", departure, size).wait_send()

    loads = [0]

    def load(src, dst):
        copy = pltpu.make_async_copy(src, dst, lsem.at[loads[0]])
        loads[0] += 1
        copy.start()
        return copy

    def cols(p):
        return pl.ds(p * PART, PART)

    def at(buf, p, fixed):
        return buf.at[tuple(fixed.get(a, slice(None)) for a in AXES) + (slice(None), cols(p))]

    barrier = pltpu.get_barrier_semaphore()
    others = [(lax.rem(t + j, 16), b) for j in range(1, 16)]
    for device in [peer(axis, step) for axis in AXES for step in (1, 2, 3)] + [partner]:
        pl.semaphore_signal(barrier, inc=1, device_id=device, device_id_type=MESH)
    l_fr = load(frames, fr)
    l_k = load(wk, k_w)
    l_v = load(wv, v_w)
    l_dn = load(wdn, dn.at[y, z, x])
    l_up = load(wup, up.at[y, z, x])
    l_q = load(wq, q_w)
    wexp[...] = jnp.zeros_like(wexp)
    wexp[pl.ds(0, BITS), :] = w_exp[...]
    bit = lax.broadcasted_iota(jnp.int32, (PADBITS, BLOCK), 0)
    offset = jnp.zeros((PADBITS, BLOCK), F32)
    for i in range(BITS):
        offset = jnp.where(bit == i, bias[i], offset)
    zt[...] = offset
    pl.semaphore_wait(barrier, 10)

    shards = {"up": (wup, up), "dn": (wdn, dn)}

    def half(buf, p, axis, n, h):
        fixed = {a: slice(None) for a in AXES}
        fixed[axis] = n
        fixed[ORDER[p][0]] = pl.ds(2 * h, 2)
        return at(buf, p, fixed)

    for m in ("up", "dn"):
        src, buf = shards[m]
        for p in range(3):
            for step in (2, 1, 3):
                dst = at(buf, p, pos)
                send(src.at[:, cols(p)], dst, peer(ORDER[p][0], step), ("ag1", m, p), "ag1")

    def gather_second(m):
        buf = shards[m][1]
        for p in range(3):
            arrived(("ag1", m, p), r3.at[0, 0])
            line = at(buf, p, {a: pos[a] for a in ORDER[p][1:]})
            for step in (2, 1, 3):
                send(line, line, peer(ORDER[p][1], step), ("ag2", m, p), "ag2")

    def gather_third(m, first):
        buf = shards[m][1]
        for p in range(3):
            axis = ORDER[p][2]
            if first:
                arrived(("ag2", m, p), r2.at[0, 0])
            for step in (1, -1):
                h = int((step == 1) != first)
                mine = half(buf, p, axis, pos[axis], h)
                send(mine, mine, peer(axis, step), ("ag3", m, p, first), ("ag3", m))

    def gather_last(m):
        buf = shards[m][1]
        for p in range(3):
            axis = ORDER[p][2]
            arrived(("ag3", m, p, True), r1.at[0, 0, 0])
            for step in (1, -1):
                block = half(buf, p, axis, shifted(axis, -step), int(step == -1))
                send(block, block, peer(axis, step), ("ag3", m, p, False), ("ag3", m))

    def gather_end(m):
        for p in range(3):
            arrived(("ag3", m, p, False), r1.at[0, 0, pl.ds(0, 2)])

    l_o = load(wo, o_w)
    l_ct = load(cot, ct.at[pl.ds(0, BLOCK)])
    l_st = load(stream, st.at[pl.ds(0, BLOCK)])
    there = pl.ds(BLOCK, BLOCK)
    send(stream, st.at[there], partner, "stream", "tokens")
    send(cot, ct.at[there], partner, "cot", "tokens")

    def project(weights, out, scale):
        def tile(i, carry):
            rows = pl.ds(pl.multiple_of(i * 256, 256), 256)
            value = nn(fr[rows, :], weights[...])
            if scale is not None:
                value = value * scale
            out[rows, :] = value.astype(BF)
            return carry

        lax.fori_loop(0, BLOCK // 256, tile, 0)

    l_fr.wait()
    l_k.wait()
    project(k_w, k, None)
    l_dn.wait()
    l_up.wait()
    gather_second("up")
    l_v.wait()
    project(v_w, v, None)

    def head_cols(h):
        return pl.ds(pl.multiple_of(h * HD, HD), HD)

    def state(h, carry):
        rows = pl.ds(pl.multiple_of(h * HD, HD), HD)
        own_state[rows, :] = tn(k[:, head_cols(h)], v[:, head_cols(h)]).astype(BF)
        return carry

    lax.fori_loop(0, HEADS, state, 0)

    def share(n):
        return pl.ds(pl.multiple_of(n * SHARE, SHARE), SHARE)

    for d in others:
        send(own_state.at[share(d[0])], a_recv.at[t], d, "a1", "a1")
    a_recv[t] = own_state[share(t), :]
    gather_second("dn")
    l_q.wait()
    project(q_w, q, 1.0 / math.sqrt(HD))
    def local_rows(r):
        width = (r + 1) * 256
        keep = (
            lax.broadcasted_iota(jnp.int32, (256, width), 0) + r * 256
            >= lax.broadcasted_iota(jnp.int32, (256, width), 1)
        )

        def local(h, carry):
            hc = head_cols(h)
            s = nt(q[pl.ds(r * 256, 256), hc], k[pl.ds(0, width), hc])
            s = jnp.where(keep, s, 0.0).astype(BF)
            mix[pl.ds(r * 256, 256), hc] = nn(s, v[pl.ds(0, width), hc])
            return carry

        lax.fori_loop(0, HEADS, local, 0)

    local_rows(0)
    arrived("a1", prefix.at[pl.ds(0, 15)])
    running = jnp.zeros((SHARE, HD), F32)
    for n in range(16):
        prefix[n] = running.astype(BF)
        if n < 15:
            running = running + a_recv[n].astype(F32)
    for d in others:
        send(prefix.at[d[0]], history.at[share(t)], d, "a2", "a2")
    history[share(t), :] = prefix[t]

    gather_third("up", True)
    gather_third("up", False)
    local_rows(1)
    gather_third("dn", True)

    arrived("a2", prefix.at[pl.ds(0, 15)])
    l_o.wait()

    def carry_in(h, carry):
        hc = head_cols(h)
        m = mix[:, hc] + nn(q[:, hc], history[hc, :])
        meansq = jnp.mean(m * m, axis=-1, keepdims=True)
        q[:, hc] = (m * lax.rsqrt(meansq + EPSILON)).astype(BF)
        return carry

    lax.fori_loop(0, HEADS, carry_in, 0)

    def out_tile(i, carry):
        rows = pl.ds(pl.multiple_of(i * 256, 256), 256)
        hid[rows, :] = (fr[rows, :].astype(F32) + nn(q[rows, :], o_w[...])).astype(BF)
        return carry

    lax.fori_loop(0, 2, out_tile, 0)
    zt[pl.ds(0, BITS), :] += nt(w_code[...], hid[...])
    zvals = zt[...]
    code[0] = jnp.tanh(zvals).astype(BF)
    send(code.at[0], code.at[1], partner, "code", "code")

    gather_last("up")
    gather_third("dn", False)

    def sums(slot):
        zv = zt[...]
        two = 2.0 * zv
        logp = jax.nn.log_sigmoid(two)
        logq = jax.nn.log_sigmoid(-two)
        prob = jax.nn.sigmoid(two)
        entropy = -(prob * logp + (1.0 - prob) * logq)
        row = lax.broadcasted_iota(jnp.int32, (PADBITS, 1), 0)
        probs = jnp.sum(prob, axis=1, keepdims=True)
        ents = jnp.sum(entropy, axis=1, keepdims=True)
        ent = jnp.sum(jnp.where(row < BITS, ents, 0.0), axis=0, keepdims=True)
        tile = jnp.where(row < BITS, probs, jnp.where(row == 24, ent, 0.0))
        ps[0, slot] = jnp.broadcast_to(tile, (PADBITS, 128))

    sums(c)
    send(ps.at[0, c], ps.at[0, c], partner, ("ps", 0), ("ps", 0))

    l_ct.wait()
    l_st.wait()
    arrived("stream", st.at[there])

    def expand(slot):
        def tile(i, carry):
            tok = pl.multiple_of(i * 256, 256)
            rows = pl.ds(slot * BLOCK + tok, 256)
            grown = tn(code[slot, :, pl.ds(tok, 256)], wexp[...])
            st[rows, :] = (st[rows, :].astype(F32) + grown).astype(BF)
            return carry

        lax.fori_loop(0, 2, tile, 0)

    expand(0)
    arrived("code", code.at[1])
    expand(1)
    gather_last("dn")

    def ps_send(stage, axis, value):
        ps[stage, pos[axis]] = value
        mine = ps.at[stage, pos[axis]]
        for step in (1, 2, 3):
            send(mine, mine, peer(axis, step), ("ps", stage), ("ps", stage))

    def ps_sum(stage):
        arrived(("ps", stage), ps.at[stage, pl.ds(0, 3)])
        return ps[stage, 0] + ps[stage, 1] + ps[stage, 2] + ps[stage, 3]

    arrived(("ps", 0), ps.at[0, 0])
    ps_send(1, "x", ps[0, 0] + ps[0, 1])

    gather_end("up")

    up_all = up.reshape(UNITS, D)
    dn_all = dn.reshape(UNITS, D)
    tiles = [pl.ds(i * 256, 256) for i in range(4)]
    coeff = math.sqrt(2.0 / math.pi)
    buffers = (pre_a, pre_b)

    def act_slabs(rows, pre):
        for j in range(UNITS // 64):
            us = pl.ds(j * 64, 64)
            val = pre[us, :]
            square = val * val
            half_t = 0.5 * jnp.tanh(val * (square * (coeff * 0.044715) + coeff)) + 0.5
            gelu = val * half_t
            act[us, rows] = gelu.astype(BF)
            slope[us, rows] = half_t + gelu * (1.0 - half_t) * (
                square * (6.0 * 0.044715 * coeff) + 2.0 * coeff
            )

    for i in range(5):
        if i < 4:
            buffers[i % 2][...] = nt(up_all[...], st[tiles[i], :])
        if i > 0:
            act_slabs(tiles[i - 1], buffers[(i - 1) % 2])

    def dpre_all():
        for i in range(5):
            if i < 4:
                buffers[i % 2][...] = nt(dn_all[...], ct[tiles[i], :])
            if i > 0:
                for j in range(UNITS // 64):
                    us = pl.ds(j * 64, 64)
                    dpre[us, tiles[i - 1]] = (
                        buffers[(i - 1) % 2][us, :] * slope[us, tiles[i - 1]]
                    ).astype(BF)

    gd_all = gd.reshape(UNITS, D)
    gu_all = gu.reshape(UNITS, D)

    def gradient(left, right, out, p):
        def tile(i, carry):
            cs = pl.ds(pl.multiple_of(p * PART + i * 256, 256), 256)
            out[:, cs] = nn(left[...], right[:, cs]).astype(BF)
            return carry

        lax.fori_loop(0, PART // 256, tile, 0)

    grads = (gd, gu)

    def landing(m, p, slot, h):
        if p == 0:
            return r1.at[m, p, slot, :, pl.ds(2 * h, 2)]
        return r1.at[m, p, slot, pl.ds(2 * h, 2)] if p == 1 else r1.at[m, p, slot, pl.ds(2 * h, 2)]

    def first_sends(m, p):
        axis = ORDER[p][2]
        for step in (1, -1):
            h = int(step == -1)
            block = half(grads[m], p, axis, shifted(axis, 2), h)
            send(block, landing(m, p, 0, h), peer(axis, step), ("far", m, p), ("rs1", m))
        for step in (1, -1):
            h = int(step == 1)
            slot = 1 if step == 1 else 2
            block = half(grads[m], p, axis, shifted(axis, step), h)
            send(block, landing(m, p, slot, h), peer(axis, step), ("near", m, p), ("rs1", m))

    def forward_sum(m, p):
        axis = ORDER[p][2]
        arrived(("far", m, p), r1.at[m, p, 0])
        for step in (1, -1):
            h = int(step == -1)
            slot = 1 if step == 1 else 2
            block = half(grads[m], p, axis, shifted(axis, step), h)
            came = landing(m, p, 0, h)
            block[...] = (block[...].astype(F32) + came[...].astype(F32)).astype(BF)
            send(block, landing(m, p, slot, h), peer(axis, step), ("near", m, p), ("rs1", m))

    def second_sends(m, p):
        axis = ORDER[p][2]
        arrived(("near", m, p), r1.at[m, p, pl.ds(1, 2)])
        block = at(grads[m], p, {axis: pos[axis]})

        def total1(i, carry):
            s1[m, p, i] = (
                block[i].astype(F32)
                + r1[m, p, 1, i].astype(F32)
                + r1[m, p, 2, i].astype(F32)
            ).astype(BF)
            return carry

        lax.fori_loop(0, 4, total1, 0)
        axis = ORDER[p][1]
        for step in (2, 1, 3):
            n = shifted(axis, step)
            src = s1.at[m, p, n] if p == 0 else s1.at[m, p, :, n]
            send(src, r2.at[m, p, step - 1], peer(axis, step), ("rs2", m, p), "rs2")

    def third_sends(m, p):
        axis = ORDER[p][1]
        arrived(("rs2", m, p), r2.at[m, p])
        mine = s1.at[m, p, pos[axis]] if p == 0 else s1.at[m, p, :, pos[axis]]
        total = mine[...].astype(F32)
        for step in range(3):
            total = total + r2[m, p, step].astype(F32)
        s2[m, p] = total.astype(BF)
        axis = ORDER[p][0]
        for step in (2, 1, 3):
            src = s2.at[m, p, shifted(axis, step)]
            send(src, r3.at[m, p, step - 1], peer(axis, step), ("rs3", m, p), "rs3")

    scale = 1.0 / math.sqrt(TOTAL)

    def last_sum(m, p):
        axis = ORDER[p][0]
        total = s2[m, p, pos[axis]].astype(F32)
        arrived(("rs3", m, p), r3.at[m, p])
        for step in range(3):
            total = total + r3[m, p, step].astype(F32)
        grad_out[pl.ds(16 * (1 - m), 16), cols(p)] = total * scale

    arrived("cot", ct.at[there])
    for p in range(3):
        gradient(act, ct, gd_all, p)
        first_sends(0, p)
    gather_end("dn")
    dpre_all()
    for p in range(3):
        forward_sum(0, p)
    for p in range(3):
        gradient(dpre, st, gu_all, p)
        first_sends(1, p)
    ps_send(2, "y", ps_sum(1))
    back = nt(wexp[...], up_all[...]).astype(BF)

    for i in range(4):
        dc[:, tiles[i]] = nn(back, dpre[:, tiles[i]])
    send(dc.at[:, there], dc_recv, partner, "dc", "dc")
    ps_send(3, "z", ps_sum(2))

    for p in range(3):
        second_sends(0, p)
    for p in range(3):
        forward_sum(1, p)
    for p in range(3):
        third_sends(0, p)
    for p in range(3):
        second_sends(1, p)

    arrived("dc", dc_recv)
    sums_all = ps_sum(3)
    row = lax.broadcasted_iota(jnp.int32, (PADBITS, 128), 0)
    pbar = jnp.where(row < BITS, sums_all / TOTAL, 0.5)
    lp, lq = jnp.log(pbar), jnp.log(1.0 - pbar)
    spread = jnp.where(row < BITS, -(pbar * lp + (1.0 - pbar) * lq), 0.0)
    batch_ent = jnp.sum(spread, axis=0, keepdims=True)
    pen_out[...] = (sums_all[24:25, :] / TOTAL - batch_ent)[:, :1]
    zv = zt[...]
    smooth = jnp.tanh(zv)
    prob = jax.nn.sigmoid(2.0 * zv)
    dcodes = nt(wexp[...], ct[pl.ds(0, BLOCK), :]) + dc[:, pl.ds(0, BLOCK)] + dc_recv[...]
    fg = dcodes * (1.0 - smooth * smooth) + ENT_WEIGHT * 2.0 * prob * (1.0 - prob) * (
        -2.0 * zv - lq[:, :1] + lp[:, :1]
    )
    for i in range(BITS):
        fg_out[i] = fg[i : i + 1, :]

    for p in range(3):
        last_sum(0, p)
    for p in range(3):
        third_sends(1, p)
    for p in range(3):
        last_sum(1, p)
    for departure, size in (
        ("ag1", r3), ("ag2", r2), (("ag3", "up"), r1.at[0]), (("ag3", "dn"), r1.at[0]),
        ("tokens", ct), ("a1", prefix.at[pl.ds(0, 15)]), ("a2", prefix.at[pl.ds(0, 15)]),
        ("code", code.at[0]), (("ps", 0), ps.at[0, 0]), (("ps", 1), ps.at[1, pl.ds(0, 3)]),
        (("ps", 2), ps.at[2, pl.ds(0, 3)]), (("ps", 3), ps.at[3, pl.ds(0, 3)]), ("dc", dc_recv),
        (("rs1", 0), r1.at[0]), (("rs1", 1), r1.at[1]), ("rs2", r2), ("rs3", r3),
    ):
        departed(departure, size)
    assert (len(arrivals), len(departures)) == (ARRIVALS, DEPARTURES), (len(arrivals), len(departures))


def body(
    frames, w_query, w_key, w_value, w_out, w_code, code_bias, w_expand, w_up, w_down,
    decoder_stream, cotangent,
):
    anywhere = pl.BlockSpec(memory_space=pl.ANY)
    smem = pl.BlockSpec(memory_space=pltpu.SMEM)
    vmem = pl.BlockSpec(memory_space=pltpu.VMEM)
    scratch = [
        pltpu.VMEM((BLOCK, D), BF),
        pltpu.VMEM((D, INNER), BF),
        pltpu.VMEM((D, INNER), BF),
        pltpu.VMEM((D, INNER), BF),
        pltpu.VMEM((INNER, D), BF),
        pltpu.VMEM((2 * BLOCK, D), BF),
        pltpu.VMEM((2 * BLOCK, D), BF),
        pltpu.VMEM((4, 4, 4, 16, D), BF),
        pltpu.VMEM((4, 4, 4, 16, D), BF),
        pltpu.VMEM((BLOCK, INNER), BF),
        pltpu.VMEM((BLOCK, INNER), BF),
        pltpu.VMEM((BLOCK, INNER), BF),
        pltpu.VMEM((BLOCK, INNER), F32),
        pltpu.VMEM((INNER, HD), BF),
        pltpu.VMEM((16, SHARE, HD), BF),
        pltpu.VMEM((16, SHARE, HD), BF),
        pltpu.VMEM((INNER, HD), BF),
        pltpu.VMEM((BLOCK, D), BF),
        pltpu.VMEM((PADBITS, BLOCK), F32),
        pltpu.VMEM((2, PADBITS, BLOCK), BF),
        pltpu.VMEM((PADBITS, 2 * BLOCK), F32),
        pltpu.VMEM((PADBITS, BLOCK), F32),
        pltpu.VMEM((PADBITS, D), BF),
        pltpu.VMEM((UNITS, 2 * BLOCK), BF),
        pltpu.VMEM((UNITS, 2 * BLOCK), BF),
        pltpu.VMEM((UNITS, 256), F32),
        pltpu.VMEM((UNITS, 256), F32),
        pltpu.VMEM((UNITS, 2 * BLOCK), F32),
        pltpu.VMEM((4, 4, 4, 16, D), BF),
        pltpu.VMEM((4, 4, 4, 16, D), BF),
        pltpu.VMEM((2, 3, 3, 4, 4, 16, PART), BF),
        pltpu.VMEM((2, 3, 4, 4, 16, PART), BF),
        pltpu.VMEM((2, 3, 3, 4, 16, PART), BF),
        pltpu.VMEM((2, 3, 4, 16, PART), BF),
        pltpu.VMEM((2, 3, 3, 16, PART), BF),
        pltpu.VMEM((4, 4, PADBITS, 128), F32),
        pltpu.SemaphoreType.DMA((16,)),
        pltpu.SemaphoreType.DMA((DEPARTURES,)),
        pltpu.SemaphoreType.DMA((ARRIVALS,)),
    ]
    grads, fg, pen = pl.pallas_call(
        fused,
        out_shape=(
            jax.ShapeDtypeStruct((32, D), F32),
            jax.ShapeDtypeStruct((BITS, 1, BLOCK), F32),
            jax.ShapeDtypeStruct((1, 1), F32),
        ),
        in_specs=[anywhere] * 5 + [vmem, smem, vmem] + [anywhere] * 4,
        out_specs=(vmem,) * 3,
        scratch_shapes=scratch,
        compiler_params=pltpu.CompilerParams(
            collective_id=0, has_side_effects=True, vmem_limit_bytes=60 * 1024 * 1024
        ),
    )(
        frames.reshape(BLOCK, D), w_query, w_key, w_value, w_out, w_code.T, code_bias, w_expand,
        w_up, w_down, decoder_stream.reshape(BLOCK, D), cotangent.reshape(BLOCK, D),
    )
    return grads[:16], grads[16:], jnp.transpose(fg, (1, 2, 0)), pen[0, 0]


def solution(mesh):
    in_specs = (
        P("batch", "tm", None),
        P(),
        P(),
        P(),
        P(),
        P(),
        P(),
        P(),
        P(("tm", "batch"), None),
        P(("tm", "batch"), None),
        P("batch", "tm", None),
        P("batch", "tm", None),
    )
    out_specs = (P(("tm", "batch"), None), P(("tm", "batch"), None), P("batch", "tm", None), P())
    return jax.shard_map(body, mesh=mesh, in_specs=in_specs, out_specs=out_specs, check_vma=False)
```

```python
import math

import jax
import jax.numpy as jnp
from jax import lax
from jax.experimental import pallas as pl
from jax.experimental.pallas import tpu as pltpu
from jax.sharding import PartitionSpec as P

HEADS = 6
HD = 128
BITS = 18
PADBITS = 32
BLOCK = 512
D = 1536
INNER = HEADS * HD
UNITS = 1024
PART = 512
EPSILON = 1e-05
ENT_WEIGHT = 2.0
TOTAL = 65536
MESH = pl.DeviceIdType.MESH
BF = jnp.bfloat16
F32 = jnp.float32

ORDER = (("x", "y", "z"), ("y", "z", "x"), ("z", "x", "y"))
AXES = ("y", "z", "x")
ARRIVALS = 58
DEPARTURES = 17
SHARE = INNER // 16


def nn(a, b):
    return jnp.dot(a, b, preferred_element_type=F32)


def nt(a, b):
    return lax.dot_general(a, b, (((1,), (1,)), ((), ())), preferred_element_type=F32)


def tn(a, b):
    return lax.dot_general(a, b, (((0,), (0,)), ((), ())), preferred_element_type=F32)


def fused(
    frames, wq, wk, wv, wo, w_code, bias, w_exp, wup, wdn, stream, cot,
    grad_out, fg_out, pen_out,
    fr, q_w, k_w, v_w, o_w, st, ct, up, dn, q, k, v, mix,
    own_state, a_recv, prefix, history, hid, zt, code, dc, dc_recv,
    wexp, act, dpre, pre_a, pre_b, slope, gd, gu, r1, s1, r2, s2, r3, ps,
    lsem, ssem, rsem,
):
    t = lax.axis_index("tm")
    b = lax.axis_index("batch")
    y, z = lax.div(t, 4), lax.rem(t, 4)
    x, c = lax.div(b, 2), lax.rem(b, 2)
    pos = {"y": y, "z": z, "x": x}

    def shifted(axis, step):
        return lax.rem(pos[axis] + step + 4, 4)

    def peer(axis, step):
        n = shifted(axis, step)
        if axis == "x":
            return (t, n * 2 + c)
        if axis == "y":
            return (n * 4 + z, b)
        return (y * 4 + n, b)

    partner = (t, x * 2 + 1 - c)
    arrivals, departures = {}, {}

    def semaphores(arrival, departure):
        return (
            ssem.at[departures.setdefault(departure, len(departures))],
            rsem.at[arrivals.setdefault(arrival, len(arrivals))],
        )

    def send(src, dst, device, arrival, departure):
        out, into = semaphores(arrival, departure)
        pltpu.make_async_remote_copy(
            src_ref=src, dst_ref=dst, send_sem=out, recv_sem=into,
            device_id=device, device_id_type=MESH,
        ).start()

    def waiter(arrival, departure, size):
        out, into = semaphores(arrival, departure)
        return pltpu.make_async_remote_copy(
            src_ref=size, dst_ref=size, send_sem=out, recv_sem=into,
            device_id=partner, device_id_type=MESH,
        )

    def arrived(arrival, size):
        waiter(arrival, "ag1", size).wait_recv()

    def departed(departure, size):
        waiter("a1", departure, size).wait_send()

    loads = [0]

    def load(src, dst):
        copy = pltpu.make_async_copy(src, dst, lsem.at[loads[0]])
        loads[0] += 1
        copy.start()
        return copy

    def cols(p):
        return pl.ds(p * PART, PART)

    def at(buf, p, fixed):
        return buf.at[tuple(fixed.get(a, slice(None)) for a in AXES) + (slice(None), cols(p))]

    barrier = pltpu.get_barrier_semaphore()
    others = [(lax.rem(t + j, 16), b) for j in range(1, 16)]
    for device in [peer(axis, step) for axis in AXES for step in (1, 2, 3)] + [partner]:
        pl.semaphore_signal(barrier, inc=1, device_id=device, device_id_type=MESH)
    l_fr = load(frames, fr)
    l_k = load(wk, k_w)
    l_v = load(wv, v_w)
    l_dn = load(wdn, dn.at[y, z, x])
    l_up = load(wup, up.at[y, z, x])
    l_q = load(wq, q_w)
    wexp[...] = jnp.zeros_like(wexp)
    wexp[pl.ds(0, BITS), :] = w_exp[...]
    bit = lax.broadcasted_iota(jnp.int32, (PADBITS, BLOCK), 0)
    offset = jnp.zeros((PADBITS, BLOCK), F32)
    for i in range(BITS):
        offset = jnp.where(bit == i, bias[i], offset)
    zt[...] = offset
    pl.semaphore_wait(barrier, 10)

    shards = {"up": (wup, up), "dn": (wdn, dn)}

    def half(buf, p, axis, n, h):
        fixed = {a: slice(None) for a in AXES}
        fixed[axis] = n
        fixed[ORDER[p][0]] = pl.ds(2 * h, 2)
        return at(buf, p, fixed)

    for m in ("up", "dn"):
        src, buf = shards[m]
        for p in range(3):
            for step in (2, 1, 3):
                dst = at(buf, p, pos)
                send(src.at[:, cols(p)], dst, peer(ORDER[p][0], step), ("ag1", m, p), "ag1")

    def gather_second(m):
        buf = shards[m][1]
        for p in range(3):
            arrived(("ag1", m, p), r3.at[0, 0])
            line = at(buf, p, {a: pos[a] for a in ORDER[p][1:]})
            for step in (2, 1, 3):
                send(line, line, peer(ORDER[p][1], step), ("ag2", m, p), "ag2")

    def gather_third(m, first):
        buf = shards[m][1]
        for p in range(3):
            axis = ORDER[p][2]
            if first:
                arrived(("ag2", m, p), r2.at[0, 0])
            for step in (1, -1):
                h = int((step == 1) != first)
                mine = half(buf, p, axis, pos[axis], h)
                send(mine, mine, peer(axis, step), ("ag3", m, p, first), ("ag3", m))

    def gather_last(m):
        buf = shards[m][1]
        for p in range(3):
            axis = ORDER[p][2]
            arrived(("ag3", m, p, True), r1.at[0, 0, 0])
            for step in (1, -1):
                block = half(buf, p, axis, shifted(axis, -step), int(step == -1))
                send(block, block, peer(axis, step), ("ag3", m, p, False), ("ag3", m))

    def gather_end(m):
        for p in range(3):
            arrived(("ag3", m, p, False), r1.at[0, 0, pl.ds(0, 2)])

    l_o = load(wo, o_w)
    l_ct = load(cot, ct.at[pl.ds(0, BLOCK)])
    l_st = load(stream, st.at[pl.ds(0, BLOCK)])
    there = pl.ds(BLOCK, BLOCK)
    send(stream, st.at[there], partner, "stream", "tokens")
    send(cot, ct.at[there], partner, "cot", "tokens")

    def project(weights, out, scale):
        def tile(i, carry):
            rows = pl.ds(pl.multiple_of(i * 256, 256), 256)
            value = nn(fr[rows, :], weights[...])
            if scale is not None:
                value = value * scale
            out[rows, :] = value.astype(BF)
            return carry

        lax.fori_loop(0, BLOCK // 256, tile, 0)

    l_fr.wait()
    l_k.wait()
    project(k_w, k, None)
    l_dn.wait()
    l_up.wait()
    gather_second("up")
    l_v.wait()
    project(v_w, v, None)

    def head_cols(h):
        return pl.ds(pl.multiple_of(h * HD, HD), HD)

    def state(h, carry):
        rows = pl.ds(pl.multiple_of(h * HD, HD), HD)
        own_state[rows, :] = tn(k[:, head_cols(h)], v[:, head_cols(h)]).astype(BF)
        return carry

    lax.fori_loop(0, HEADS, state, 0)

    def share(n):
        return pl.ds(pl.multiple_of(n * SHARE, SHARE), SHARE)

    for d in others:
        send(own_state.at[share(d[0])], a_recv.at[t], d, "a1", "a1")
    a_recv[t] = own_state[share(t), :]
    gather_second("dn")
    l_q.wait()
    project(q_w, q, 1.0 / math.sqrt(HD))
    def local_rows(r):
        width = (r + 1) * 256
        keep = (
            lax.broadcasted_iota(jnp.int32, (256, width), 0) + r * 256
            >= lax.broadcasted_iota(jnp.int32, (256, width), 1)
        )

        def local(h, carry):
            hc = head_cols(h)
            s = nt(q[pl.ds(r * 256, 256), hc], k[pl.ds(0, width), hc])
            s = jnp.where(keep, s, 0.0).astype(BF)
            mix[pl.ds(r * 256, 256), hc] = nn(s, v[pl.ds(0, width), hc])
            return carry

        lax.fori_loop(0, HEADS, local, 0)

    local_rows(0)
    arrived("a1", prefix.at[pl.ds(0, 15)])
    running = jnp.zeros((SHARE, HD), F32)
    for n in range(16):
        prefix[n] = running.astype(BF)
        if n < 15:
            running = running + a_recv[n].astype(F32)
    for d in others:
        send(prefix.at[d[0]], history.at[share(t)], d, "a2", "a2")
    history[share(t), :] = prefix[t]

    gather_third("up", True)
    gather_third("up", False)
    local_rows(1)
    gather_third("dn", True)

    arrived("a2", prefix.at[pl.ds(0, 15)])
    l_o.wait()

    def carry_in(h, carry):
        hc = head_cols(h)
        m = mix[:, hc] + nn(q[:, hc], history[hc, :])
        meansq = jnp.mean(m * m, axis=-1, keepdims=True)
        q[:, hc] = (m * lax.rsqrt(meansq + EPSILON)).astype(BF)
        return carry

    lax.fori_loop(0, HEADS, carry_in, 0)

    def out_tile(i, carry):
        rows = pl.ds(pl.multiple_of(i * 256, 256), 256)
        hid[rows, :] = (fr[rows, :].astype(F32) + nn(q[rows, :], o_w[...])).astype(BF)
        return carry

    lax.fori_loop(0, 2, out_tile, 0)
    zt[pl.ds(0, BITS), :] += nt(w_code[...], hid[...])
    zvals = zt[...]
    code[0] = jnp.tanh(zvals).astype(BF)
    send(code.at[0], code.at[1], partner, "code", "code")

    gather_last("up")
    gather_third("dn", False)

    def sums(slot):
        zv = zt[...]
        two = 2.0 * zv
        logp = jax.nn.log_sigmoid(two)
        logq = jax.nn.log_sigmoid(-two)
        prob = jax.nn.sigmoid(two)
        entropy = -(prob * logp + (1.0 - prob) * logq)
        row = lax.broadcasted_iota(jnp.int32, (PADBITS, 1), 0)
        probs = jnp.sum(prob, axis=1, keepdims=True)
        ents = jnp.sum(entropy, axis=1, keepdims=True)
        ent = jnp.sum(jnp.where(row < BITS, ents, 0.0), axis=0, keepdims=True)
        tile = jnp.where(row < BITS, probs, jnp.where(row == 24, ent, 0.0))
        ps[0, slot] = jnp.broadcast_to(tile, (PADBITS, 128))

    sums(c)
    send(ps.at[0, c], ps.at[0, c], partner, ("ps", 0), ("ps", 0))

    l_ct.wait()
    l_st.wait()
    arrived("stream", st.at[there])

    def expand(slot):
        def tile(i, carry):
            tok = pl.multiple_of(i * 256, 256)
            rows = pl.ds(slot * BLOCK + tok, 256)
            grown = tn(code[slot, :, pl.ds(tok, 256)], wexp[...])
            st[rows, :] = (st[rows, :].astype(F32) + grown).astype(BF)
            return carry

        lax.fori_loop(0, 2, tile, 0)

    expand(0)
    arrived("code", code.at[1])
    expand(1)
    gather_last("dn")

    def ps_send(stage, axis, value):
        ps[stage, pos[axis]] = value
        mine = ps.at[stage, pos[axis]]
        for step in (1, 2, 3):
            send(mine, mine, peer(axis, step), ("ps", stage), ("ps", stage))

    def ps_sum(stage):
        arrived(("ps", stage), ps.at[stage, pl.ds(0, 3)])
        return ps[stage, 0] + ps[stage, 1] + ps[stage, 2] + ps[stage, 3]

    arrived(("ps", 0), ps.at[0, 0])
    ps_send(1, "x", ps[0, 0] + ps[0, 1])

    gather_end("up")

    up_all = up.reshape(UNITS, D)
    dn_all = dn.reshape(UNITS, D)
    tiles = [pl.ds(i * 256, 256) for i in range(4)]
    coeff = math.sqrt(2.0 / math.pi)
    buffers = (pre_a, pre_b)

    def act_slabs(rows, pre):
        for j in range(UNITS // 64):
            us = pl.ds(j * 64, 64)
            val = pre[us, :]
            square = val * val
            half_t = 0.5 * jnp.tanh(val * (square * (coeff * 0.044715) + coeff)) + 0.5
            gelu = val * half_t
            act[us, rows] = gelu.astype(BF)
            slope[us, rows] = half_t + gelu * (1.0 - half_t) * (
                square * (6.0 * 0.044715 * coeff) + 2.0 * coeff
            )

    for i in range(5):
        if i < 4:
            buffers[i % 2][...] = nt(up_all[...], st[tiles[i], :])
        if i > 0:
            act_slabs(tiles[i - 1], buffers[(i - 1) % 2])

    def dpre_all():
        for i in range(5):
            if i < 4:
                buffers[i % 2][...] = nt(dn_all[...], ct[tiles[i], :])
            if i > 0:
                for j in range(UNITS // 64):
                    us = pl.ds(j * 64, 64)
                    dpre[us, tiles[i - 1]] = (
                        buffers[(i - 1) % 2][us, :] * slope[us, tiles[i - 1]]
                    ).astype(BF)

    gd_all = gd.reshape(UNITS, D)
    gu_all = gu.reshape(UNITS, D)

    def gradient(left, right, out, p):
        def tile(i, carry):
            cs = pl.ds(pl.multiple_of(p * PART + i * 256, 256), 256)
            out[:, cs] = nn(left[...], right[:, cs]).astype(BF)
            return carry

        lax.fori_loop(0, PART // 256, tile, 0)

    grads = (gd, gu)

    def landing(m, p, slot, h):
        if p == 0:
            return r1.at[m, p, slot, :, pl.ds(2 * h, 2)]
        return r1.at[m, p, slot, pl.ds(2 * h, 2)] if p == 1 else r1.at[m, p, slot, pl.ds(2 * h, 2)]

    def first_sends(m, p):
        axis = ORDER[p][2]
        for step in (1, -1):
            h = int(step == -1)
            block = half(grads[m], p, axis, shifted(axis, 2), h)
            send(block, landing(m, p, 0, h), peer(axis, step), ("far", m, p), ("rs1", m))
        for step in (1, -1):
            h = int(step == 1)
            slot = 1 if step == 1 else 2
            block = half(grads[m], p, axis, shifted(axis, step), h)
            send(block, landing(m, p, slot, h), peer(axis, step), ("near", m, p), ("rs1", m))

    def forward_sum(m, p):
        axis = ORDER[p][2]
        arrived(("far", m, p), r1.at[m, p, 0])
        for step in (1, -1):
            h = int(step == -1)
            slot = 1 if step == 1 else 2
            block = half(grads[m], p, axis, shifted(axis, step), h)
            came = landing(m, p, 0, h)
            block[...] = (block[...].astype(F32) + came[...].astype(F32)).astype(BF)
            send(block, landing(m, p, slot, h), peer(axis, step), ("near", m, p), ("rs1", m))

    def second_sends(m, p):
        axis = ORDER[p][2]
        arrived(("near", m, p), r1.at[m, p, pl.ds(1, 2)])
        block = at(grads[m], p, {axis: pos[axis]})

        def total1(i, carry):
            s1[m, p, i] = (
                block[i].astype(F32)
                + r1[m, p, 1, i].astype(F32)
                + r1[m, p, 2, i].astype(F32)
            ).astype(BF)
            return carry

        lax.fori_loop(0, 4, total1, 0)
        axis = ORDER[p][1]
        for step in (2, 1, 3):
            n = shifted(axis, step)
            src = s1.at[m, p, n] if p == 0 else s1.at[m, p, :, n]
            send(src, r2.at[m, p, step - 1], peer(axis, step), ("rs2", m, p), "rs2")

    def third_sends(m, p):
        axis = ORDER[p][1]
        arrived(("rs2", m, p), r2.at[m, p])
        mine = s1.at[m, p, pos[axis]] if p == 0 else s1.at[m, p, :, pos[axis]]
        total = mine[...].astype(F32)
        for step in range(3):
            total = total + r2[m, p, step].astype(F32)
        s2[m, p] = total.astype(BF)
        axis = ORDER[p][0]
        for step in (2, 1, 3):
            src = s2.at[m, p, shifted(axis, step)]
            send(src, r3.at[m, p, step - 1], peer(axis, step), ("rs3", m, p), "rs3")

    scale = 1.0 / math.sqrt(TOTAL)

    def last_sum(m, p):
        axis = ORDER[p][0]
        total = s2[m, p, pos[axis]].astype(F32)
        arrived(("rs3", m, p), r3.at[m, p])
        for step in range(3):
            total = total + r3[m, p, step].astype(F32)
        grad_out[pl.ds(16 * (1 - m), 16), cols(p)] = total * scale

    arrived("cot", ct.at[there])
    for p in range(3):
        gradient(act, ct, gd_all, p)
        first_sends(0, p)
    gather_end("dn")
    dpre_all()
    for p in range(3):
        gradient(dpre, st, gu_all, p)
        forward_sum(0, p)
        first_sends(1, p)
    ps_send(2, "y", ps_sum(1))
    back = nt(wexp[...], up_all[...]).astype(BF)

    for i in range(4):
        dc[:, tiles[i]] = nn(back, dpre[:, tiles[i]])
    send(dc.at[:, there], dc_recv, partner, "dc", "dc")
    ps_send(3, "z", ps_sum(2))

    for p in range(3):
        second_sends(0, p)
    for p in range(3):
        forward_sum(1, p)
    for p in range(3):
        third_sends(0, p)
    for p in range(3):
        second_sends(1, p)

    arrived("dc", dc_recv)
    sums_all = ps_sum(3)
    row = lax.broadcasted_iota(jnp.int32, (PADBITS, 128), 0)
    pbar = jnp.where(row < BITS, sums_all / TOTAL, 0.5)
    lp, lq = jnp.log(pbar), jnp.log(1.0 - pbar)
    spread = jnp.where(row < BITS, -(pbar * lp + (1.0 - pbar) * lq), 0.0)
    batch_ent = jnp.sum(spread, axis=0, keepdims=True)
    pen_out[...] = (sums_all[24:25, :] / TOTAL - batch_ent)[:, :1]
    zv = zt[...]
    smooth = jnp.tanh(zv)
    prob = jax.nn.sigmoid(2.0 * zv)
    dcodes = nt(wexp[...], ct[pl.ds(0, BLOCK), :]) + dc[:, pl.ds(0, BLOCK)] + dc_recv[...]
    fg = dcodes * (1.0 - smooth * smooth) + ENT_WEIGHT * 2.0 * prob * (1.0 - prob) * (
        -2.0 * zv - lq[:, :1] + lp[:, :1]
    )
    for i in range(BITS):
        fg_out[i] = fg[i : i + 1, :]

    for p in range(3):
        last_sum(0, p)
    for p in range(3):
        third_sends(1, p)
    for p in range(3):
        last_sum(1, p)
    for departure, size in (
        ("ag1", r3), ("ag2", r2), (("ag3", "up"), r1.at[0]), (("ag3", "dn"), r1.at[0]),
        ("tokens", ct), ("a1", prefix.at[pl.ds(0, 15)]), ("a2", prefix.at[pl.ds(0, 15)]),
        ("code", code.at[0]), (("ps", 0), ps.at[0, 0]), (("ps", 1), ps.at[1, pl.ds(0, 3)]),
        (("ps", 2), ps.at[2, pl.ds(0, 3)]), (("ps", 3), ps.at[3, pl.ds(0, 3)]), ("dc", dc_recv),
        (("rs1", 0), r1.at[0]), (("rs1", 1), r1.at[1]), ("rs2", r2), ("rs3", r3),
    ):
        departed(departure, size)
    assert (len(arrivals), len(departures)) == (ARRIVALS, DEPARTURES), (len(arrivals), len(departures))


def body(
    frames, w_query, w_key, w_value, w_out, w_code, code_bias, w_expand, w_up, w_down,
    decoder_stream, cotangent,
):
    anywhere = pl.BlockSpec(memory_space=pl.ANY)
    smem = pl.BlockSpec(memory_space=pltpu.SMEM)
    vmem = pl.BlockSpec(memory_space=pltpu.VMEM)
    scratch = [
        pltpu.VMEM((BLOCK, D), BF),
        pltpu.VMEM((D, INNER), BF),
        pltpu.VMEM((D, INNER), BF),
        pltpu.VMEM((D, INNER), BF),
        pltpu.VMEM((INNER, D), BF),
        pltpu.VMEM((2 * BLOCK, D), BF),
        pltpu.VMEM((2 * BLOCK, D), BF),
        pltpu.VMEM((4, 4, 4, 16, D), BF),
        pltpu.VMEM((4, 4, 4, 16, D), BF),
        pltpu.VMEM((BLOCK, INNER), BF),
        pltpu.VMEM((BLOCK, INNER), BF),
        pltpu.VMEM((BLOCK, INNER), BF),
        pltpu.VMEM((BLOCK, INNER), F32),
        pltpu.VMEM((INNER, HD), BF),
        pltpu.VMEM((16, SHARE, HD), BF),
        pltpu.VMEM((16, SHARE, HD), BF),
        pltpu.VMEM((INNER, HD), BF),
        pltpu.VMEM((BLOCK, D), BF),
        pltpu.VMEM((PADBITS, BLOCK), F32),
        pltpu.VMEM((2, PADBITS, BLOCK), BF),
        pltpu.VMEM((PADBITS, 2 * BLOCK), F32),
        pltpu.VMEM((PADBITS, BLOCK), F32),
        pltpu.VMEM((PADBITS, D), BF),
        pltpu.VMEM((UNITS, 2 * BLOCK), BF),
        pltpu.VMEM((UNITS, 2 * BLOCK), BF),
        pltpu.VMEM((UNITS, 256), F32),
        pltpu.VMEM((UNITS, 256), F32),
        pltpu.VMEM((UNITS, 2 * BLOCK), F32),
        pltpu.VMEM((4, 4, 4, 16, D), BF),
        pltpu.VMEM((4, 4, 4, 16, D), BF),
        pltpu.VMEM((2, 3, 3, 4, 4, 16, PART), BF),
        pltpu.VMEM((2, 3, 4, 4, 16, PART), BF),
        pltpu.VMEM((2, 3, 3, 4, 16, PART), BF),
        pltpu.VMEM((2, 3, 4, 16, PART), BF),
        pltpu.VMEM((2, 3, 3, 16, PART), BF),
        pltpu.VMEM((4, 4, PADBITS, 128), F32),
        pltpu.SemaphoreType.DMA((16,)),
        pltpu.SemaphoreType.DMA((DEPARTURES,)),
        pltpu.SemaphoreType.DMA((ARRIVALS,)),
    ]
    grads, fg, pen = pl.pallas_call(
        fused,
        out_shape=(
            jax.ShapeDtypeStruct((32, D), F32),
            jax.ShapeDtypeStruct((BITS, 1, BLOCK), F32),
            jax.ShapeDtypeStruct((1, 1), F32),
        ),
        in_specs=[anywhere] * 5 + [vmem, smem, vmem] + [anywhere] * 4,
        out_specs=(vmem,) * 3,
        scratch_shapes=scratch,
        compiler_params=pltpu.CompilerParams(
            collective_id=0, has_side_effects=True, vmem_limit_bytes=60 * 1024 * 1024
        ),
    )(
        frames.reshape(BLOCK, D), w_query, w_key, w_value, w_out, w_code.T, code_bias, w_expand,
        w_up, w_down, decoder_stream.reshape(BLOCK, D), cotangent.reshape(BLOCK, D),
    )
    return grads[:16], grads[16:], jnp.transpose(fg, (1, 2, 0)), pen[0, 0]


def solution(mesh):
    in_specs = (
        P("batch", "tm", None),
        P(),
        P(),
        P(),
        P(),
        P(),
        P(),
        P(),
        P(("tm", "batch"), None),
        P(("tm", "batch"), None),
        P("batch", "tm", None),
        P("batch", "tm", None),
    )
    out_specs = (P(("tm", "batch"), None), P(("tm", "batch"), None), P("batch", "tm", None), P())
    return jax.shard_map(body, mesh=mesh, in_specs=in_specs, out_specs=out_specs, check_vma=False)
```

```python
import math

import jax
import jax.numpy as jnp
from jax import lax
from jax.experimental import pallas as pl
from jax.experimental.pallas import tpu as pltpu
from jax.sharding import PartitionSpec as P

HEADS = 6
HD = 128
BITS = 18
PADBITS = 32
BLOCK = 512
D = 1536
INNER = HEADS * HD
UNITS = 1024
PART = 512
EPSILON = 1e-05
ENT_WEIGHT = 2.0
TOTAL = 65536
MESH = pl.DeviceIdType.MESH
BF = jnp.bfloat16
F32 = jnp.float32

ORDER = (("x", "y", "z"), ("y", "z", "x"), ("z", "x", "y"))
AXES = ("y", "z", "x")
ARRIVALS = 70
DEPARTURES = 17
SHARE = INNER // 16


def nn(a, b):
    return jnp.dot(a, b, preferred_element_type=F32)


def nt(a, b):
    return lax.dot_general(a, b, (((1,), (1,)), ((), ())), preferred_element_type=F32)


def tn(a, b):
    return lax.dot_general(a, b, (((0,), (0,)), ((), ())), preferred_element_type=F32)


def fused(
    frames, wq, wk, wv, wo, w_code, bias, w_exp, wup, wdn, stream, cot,
    grad_out, fg_out, pen_out,
    fr, q_w, k_w, v_w, o_w, st, ct, up, dn, q, k, v, mix,
    own_state, a_recv, prefix, history, hid, zt, code, dc, dc_recv,
    wexp, act, dpre, pre_a, pre_b, slope, gd, gu, r1, s1, r2, s2, r3, ps,
    lsem, ssem, rsem,
):
    t = lax.axis_index("tm")
    b = lax.axis_index("batch")
    y, z = lax.div(t, 4), lax.rem(t, 4)
    x, c = lax.div(b, 2), lax.rem(b, 2)
    pos = {"y": y, "z": z, "x": x}

    def shifted(axis, step):
        return lax.rem(pos[axis] + step + 4, 4)

    def peer(axis, step):
        n = shifted(axis, step)
        if axis == "x":
            return (t, n * 2 + c)
        if axis == "y":
            return (n * 4 + z, b)
        return (y * 4 + n, b)

    partner = (t, x * 2 + 1 - c)
    arrivals, departures = {}, {}

    def semaphores(arrival, departure):
        return (
            ssem.at[departures.setdefault(departure, len(departures))],
            rsem.at[arrivals.setdefault(arrival, len(arrivals))],
        )

    def send(src, dst, device, arrival, departure):
        out, into = semaphores(arrival, departure)
        pltpu.make_async_remote_copy(
            src_ref=src, dst_ref=dst, send_sem=out, recv_sem=into,
            device_id=device, device_id_type=MESH,
        ).start()

    def waiter(arrival, departure, size):
        out, into = semaphores(arrival, departure)
        return pltpu.make_async_remote_copy(
            src_ref=size, dst_ref=size, send_sem=out, recv_sem=into,
            device_id=partner, device_id_type=MESH,
        )

    def arrived(arrival, size):
        waiter(arrival, "ag1", size).wait_recv()

    def departed(departure, size):
        waiter("a1", departure, size).wait_send()

    loads = [0]

    def load(src, dst):
        copy = pltpu.make_async_copy(src, dst, lsem.at[loads[0]])
        loads[0] += 1
        copy.start()
        return copy

    def cols(p):
        return pl.ds(p * PART, PART)

    def at(buf, p, fixed, lo=0, w=PART):
        place = tuple(fixed.get(a, slice(None)) for a in AXES)
        return buf.at[place + (slice(None), pl.ds(p * PART + lo, w))]

    barrier = pltpu.get_barrier_semaphore()
    others = [(lax.rem(t + j, 16), b) for j in range(1, 16)]
    for device in [peer(axis, step) for axis in AXES for step in (1, 2, 3)] + [partner]:
        pl.semaphore_signal(barrier, inc=1, device_id=device, device_id_type=MESH)
    l_fr = load(frames, fr)
    l_k = load(wk, k_w)
    l_v = load(wv, v_w)
    l_dn = load(wdn, dn.at[y, z, x])
    l_up = load(wup, up.at[y, z, x])
    l_q = load(wq, q_w)
    wexp[...] = jnp.zeros_like(wexp)
    wexp[pl.ds(0, BITS), :] = w_exp[...]
    bit = lax.broadcasted_iota(jnp.int32, (PADBITS, BLOCK), 0)
    offset = jnp.zeros((PADBITS, BLOCK), F32)
    for i in range(BITS):
        offset = jnp.where(bit == i, bias[i], offset)
    zt[...] = offset
    pl.semaphore_wait(barrier, 10)

    shards = {"up": (wup, up), "dn": (wdn, dn)}

    def half(buf, p, axis, n, h, lo=0, w=PART):
        fixed = {a: slice(None) for a in AXES}
        fixed[axis] = n
        fixed[ORDER[p][0]] = pl.ds(2 * h, 2)
        return at(buf, p, fixed, lo, w)

    for m in ("up", "dn"):
        src, buf = shards[m]
        for p in range(3):
            for step in (2, 1, 3):
                dst = at(buf, p, pos)
                send(src.at[:, cols(p)], dst, peer(ORDER[p][0], step), ("ag1", m, p), "ag1")

    def gather_second(m):
        buf = shards[m][1]
        for p in range(3):
            arrived(("ag1", m, p), r3.at[0, 0])
            line = at(buf, p, {a: pos[a] for a in ORDER[p][1:]})
            for step in (2, 1, 3):
                send(line, line, peer(ORDER[p][1], step), ("ag2", m, p), "ag2")

    def gather_third(m, first):
        buf = shards[m][1]
        for p in range(3):
            axis = ORDER[p][2]
            if first:
                arrived(("ag2", m, p), r2.at[0, 0])
            for step in (1, -1):
                h = int((step == 1) != first)
                mine = half(buf, p, axis, pos[axis], h)
                send(mine, mine, peer(axis, step), ("ag3", m, p, first), ("ag3", m))

    def gather_last(m):
        buf = shards[m][1]
        for p in range(3):
            axis = ORDER[p][2]
            arrived(("ag3", m, p, True), r1.at[0, 0, 0])
            for step in (1, -1):
                block = half(buf, p, axis, shifted(axis, -step), int(step == -1))
                send(block, block, peer(axis, step), ("ag3", m, p, False), ("ag3", m))

    def gather_end(m):
        for p in range(3):
            arrived(("ag3", m, p, False), r1.at[0, 0, pl.ds(0, 2)])

    l_o = load(wo, o_w)
    l_ct = load(cot, ct.at[pl.ds(0, BLOCK)])
    l_st = load(stream, st.at[pl.ds(0, BLOCK)])
    there = pl.ds(BLOCK, BLOCK)
    send(stream, st.at[there], partner, "stream", "tokens")
    send(cot, ct.at[there], partner, "cot", "tokens")

    def project(weights, out, scale):
        def tile(i, carry):
            rows = pl.ds(pl.multiple_of(i * 256, 256), 256)
            value = nn(fr[rows, :], weights[...])
            if scale is not None:
                value = value * scale
            out[rows, :] = value.astype(BF)
            return carry

        lax.fori_loop(0, BLOCK // 256, tile, 0)

    l_fr.wait()
    l_k.wait()
    project(k_w, k, None)
    l_dn.wait()
    l_up.wait()
    gather_second("up")
    l_v.wait()
    project(v_w, v, None)

    def head_cols(h):
        return pl.ds(pl.multiple_of(h * HD, HD), HD)

    def state(h, carry):
        rows = pl.ds(pl.multiple_of(h * HD, HD), HD)
        own_state[rows, :] = tn(k[:, head_cols(h)], v[:, head_cols(h)]).astype(BF)
        return carry

    lax.fori_loop(0, HEADS, state, 0)

    def share(n):
        return pl.ds(pl.multiple_of(n * SHARE, SHARE), SHARE)

    for d in others:
        send(own_state.at[share(d[0])], a_recv.at[t], d, "a1", "a1")
    a_recv[t] = own_state[share(t), :]
    gather_second("dn")
    l_q.wait()
    project(q_w, q, 1.0 / math.sqrt(HD))
    def local_rows(r):
        width = (r + 1) * 256
        keep = (
            lax.broadcasted_iota(jnp.int32, (256, width), 0) + r * 256
            >= lax.broadcasted_iota(jnp.int32, (256, width), 1)
        )

        def local(h, carry):
            hc = head_cols(h)
            s = nt(q[pl.ds(r * 256, 256), hc], k[pl.ds(0, width), hc])
            s = jnp.where(keep, s, 0.0).astype(BF)
            mix[pl.ds(r * 256, 256), hc] = nn(s, v[pl.ds(0, width), hc])
            return carry

        lax.fori_loop(0, HEADS, local, 0)

    local_rows(0)
    arrived("a1", prefix.at[pl.ds(0, 15)])
    running = jnp.zeros((SHARE, HD), F32)
    for n in range(16):
        prefix[n] = running.astype(BF)
        if n < 15:
            running = running + a_recv[n].astype(F32)
    for d in others:
        send(prefix.at[d[0]], history.at[share(t)], d, "a2", "a2")
    history[share(t), :] = prefix[t]

    gather_third("up", True)
    gather_third("up", False)
    local_rows(1)
    gather_third("dn", True)

    arrived("a2", prefix.at[pl.ds(0, 15)])
    l_o.wait()

    def carry_in(h, carry):
        hc = head_cols(h)
        m = mix[:, hc] + nn(q[:, hc], history[hc, :])
        meansq = jnp.mean(m * m, axis=-1, keepdims=True)
        q[:, hc] = (m * lax.rsqrt(meansq + EPSILON)).astype(BF)
        return carry

    lax.fori_loop(0, HEADS, carry_in, 0)
    def out_tile(i, carry):
        rows = pl.ds(pl.multiple_of(i * 256, 256), 256)
        hid[rows, :] = (fr[rows, :].astype(F32) + nn(q[rows, :], o_w[...])).astype(BF)
        return carry

    lax.fori_loop(0, 2, out_tile, 0)
    zt[pl.ds(0, BITS), :] += nt(w_code[...], hid[...])
    zvals = zt[...]
    code[0] = jnp.tanh(zvals).astype(BF)
    send(code.at[0], code.at[1], partner, "code", "code")


    gather_last("up")
    gather_third("dn", False)

    def sums(slot):
        zv = zt[...]
        two = 2.0 * zv
        logp = jax.nn.log_sigmoid(two)
        logq = jax.nn.log_sigmoid(-two)
        prob = jax.nn.sigmoid(two)
        entropy = -(prob * logp + (1.0 - prob) * logq)
        row = lax.broadcasted_iota(jnp.int32, (PADBITS, 1), 0)
        probs = jnp.sum(prob, axis=1, keepdims=True)
        ents = jnp.sum(entropy, axis=1, keepdims=True)
        ent = jnp.sum(jnp.where(row < BITS, ents, 0.0), axis=0, keepdims=True)
        tile = jnp.where(row < BITS, probs, jnp.where(row == 24, ent, 0.0))
        ps[0, slot] = jnp.broadcast_to(tile, (PADBITS, 128))

    sums(c)
    send(ps.at[0, c], ps.at[0, c], partner, ("ps", 0), ("ps", 0))

    l_ct.wait()
    l_st.wait()
    arrived("stream", st.at[there])

    def expand(slot):
        def tile(i, carry):
            tok = pl.multiple_of(i * 256, 256)
            rows = pl.ds(slot * BLOCK + tok, 256)
            grown = tn(code[slot, :, pl.ds(tok, 256)], wexp[...])
            st[rows, :] = (st[rows, :].astype(F32) + grown).astype(BF)
            return carry

        lax.fori_loop(0, 2, tile, 0)

    expand(0)
    arrived("code", code.at[1])
    expand(1)
    gather_last("dn")

    def ps_send(stage, axis, value):
        ps[stage, pos[axis]] = value
        mine = ps.at[stage, pos[axis]]
        for step in (1, 2, 3):
            send(mine, mine, peer(axis, step), ("ps", stage), ("ps", stage))

    def ps_sum(stage):
        arrived(("ps", stage), ps.at[stage, pl.ds(0, 3)])
        return ps[stage, 0] + ps[stage, 1] + ps[stage, 2] + ps[stage, 3]

    arrived(("ps", 0), ps.at[0, 0])
    ps_send(1, "x", ps[0, 0] + ps[0, 1])

    gather_end("up")

    up_all = up.reshape(UNITS, D)
    dn_all = dn.reshape(UNITS, D)
    tiles = [pl.ds(i * 256, 256) for i in range(4)]
    coeff = math.sqrt(2.0 / math.pi)
    buffers = (pre_a, pre_b)

    def act_slabs(rows, pre):
        for j in range(UNITS // 64):
            us = pl.ds(j * 64, 64)
            val = pre[us, :]
            square = val * val
            half_t = 0.5 * jnp.tanh(val * (square * (coeff * 0.044715) + coeff)) + 0.5
            gelu = val * half_t
            act[us, rows] = gelu.astype(BF)
            slope[us, rows] = half_t + gelu * (1.0 - half_t) * (
                square * (6.0 * 0.044715 * coeff) + 2.0 * coeff
            )

    for i in range(5):
        if i < 4:
            buffers[i % 2][...] = nt(up_all[...], st[tiles[i], :])
        if i > 0:
            act_slabs(tiles[i - 1], buffers[(i - 1) % 2])

    def dpre_all():
        for i in range(5):
            if i < 4:
                buffers[i % 2][...] = nt(dn_all[...], ct[tiles[i], :])
            if i > 0:
                for j in range(UNITS // 64):
                    us = pl.ds(j * 64, 64)
                    dpre[us, tiles[i - 1]] = (
                        buffers[(i - 1) % 2][us, :] * slope[us, tiles[i - 1]]
                    ).astype(BF)

    gd_all = gd.reshape(UNITS, D)
    gu_all = gu.reshape(UNITS, D)

    def gradient(left, right, out, p, lo, w):
        def tile(i, carry):
            cs = pl.ds(pl.multiple_of(p * PART + lo + i * 256, 256), 256)
            out[:, cs] = nn(left[...], right[:, cs]).astype(BF)
            return carry

        lax.fori_loop(0, w // 256, tile, 0)

    grads = (gd, gu)
    first_chunks = [(0, p, 0, PART) for p in range(3)]
    last_chunks = [(1, p, lo, 256) for lo in (0, 256) for p in range(3)]

    def landing(chunk, slot, h):
        m, p, lo, w = chunk
        two = pl.ds(2 * h, 2)
        place = (slice(None), two) if p == 0 else (two, slice(None))
        return r1.at[(m, p, slot) + place + (slice(None), pl.ds(lo, w))]

    def first_sends(chunk):
        m, p, lo, w = chunk
        axis = ORDER[p][2]
        for step in (1, -1):
            h = int(step == -1)
            block = half(grads[m], p, axis, shifted(axis, 2), h, lo, w)
            send(block, landing(chunk, 0, h), peer(axis, step), ("far", chunk), ("rs1", m))
        for step in (1, -1):
            h = int(step == 1)
            slot = 1 if step == 1 else 2
            block = half(grads[m], p, axis, shifted(axis, step), h, lo, w)
            send(block, landing(chunk, slot, h), peer(axis, step), ("near", chunk), ("rs1", m))

    def forward_sum(chunk):
        m, p, lo, w = chunk
        axis = ORDER[p][2]
        arrived(("far", chunk), r1.at[m, p, 0, :, :, :, pl.ds(lo, w)])
        for step in (1, -1):
            h = int(step == -1)
            slot = 1 if step == 1 else 2
            block = half(grads[m], p, axis, shifted(axis, step), h, lo, w)
            came = landing(chunk, 0, h)
            block[...] = (block[...].astype(F32) + came[...].astype(F32)).astype(BF)
            send(block, landing(chunk, slot, h), peer(axis, step), ("near", chunk), ("rs1", m))

    def second_sends(chunk):
        m, p, lo, w = chunk
        axis = ORDER[p][2]
        cs = pl.ds(lo, w)
        arrived(("near", chunk), r1.at[m, p, pl.ds(1, 2), :, :, :, cs])
        block = at(grads[m], p, {axis: pos[axis]}, lo, w)

        def total1(i, carry):
            s1[m, p, i, :, :, cs] = (
                block[i].astype(F32)
                + r1[m, p, 1, i, :, :, cs].astype(F32)
                + r1[m, p, 2, i, :, :, cs].astype(F32)
            ).astype(BF)
            return carry

        lax.fori_loop(0, 4, total1, 0)
        axis = ORDER[p][1]
        for step in (2, 1, 3):
            n = shifted(axis, step)
            src = s1.at[m, p, n, :, :, cs] if p == 0 else s1.at[m, p, :, n, :, cs]
            send(src, r2.at[m, p, step - 1, :, :, cs], peer(axis, step), ("rs2", chunk), "rs2")

    def third_sends(chunk):
        m, p, lo, w = chunk
        axis = ORDER[p][1]
        cs = pl.ds(lo, w)
        arrived(("rs2", chunk), r2.at[m, p, :, :, :, cs])
        n = pos[axis]
        mine = s1.at[m, p, n, :, :, cs] if p == 0 else s1.at[m, p, :, n, :, cs]
        total = mine[...].astype(F32)
        for step in range(3):
            total = total + r2[m, p, step, :, :, cs].astype(F32)
        s2[m, p, :, :, cs] = total.astype(BF)
        axis = ORDER[p][0]
        for step in (2, 1, 3):
            src = s2.at[m, p, shifted(axis, step), :, cs]
            send(src, r3.at[m, p, step - 1, :, cs], peer(axis, step), ("rs3", chunk), "rs3")

    scale = 1.0 / math.sqrt(TOTAL)

    def last_sum(chunk):
        m, p, lo, w = chunk
        axis = ORDER[p][0]
        cs = pl.ds(lo, w)
        total = s2[m, p, pos[axis], :, cs].astype(F32)
        arrived(("rs3", chunk), r3.at[m, p, :, :, cs])
        for step in range(3):
            total = total + r3[m, p, step, :, cs].astype(F32)
        grad_out[pl.ds(16 * (1 - m), 16), pl.ds(p * PART + lo, w)] = total * scale

    arrived("cot", ct.at[there])
    for chunk in first_chunks:
        gradient(act, ct, gd_all, *chunk[1:])
        first_sends(chunk)
    gather_end("dn")
    dpre_all()
    for i, chunk in enumerate(last_chunks):
        gradient(dpre, st, gu_all, *chunk[1:])
        if i in (1, 3, 5):
            forward_sum(first_chunks[i // 2])
        first_sends(chunk)

    ps_send(2, "y", ps_sum(1))
    back = nt(wexp[...], up_all[...]).astype(BF)
    for i in range(4):
        dc[:, tiles[i]] = nn(back, dpre[:, tiles[i]])
    send(dc.at[:, there], dc_recv, partner, "dc", "dc")
    ps_send(3, "z", ps_sum(2))

    for chunk in last_chunks[:3]:
        forward_sum(chunk)
    for chunk in first_chunks:
        second_sends(chunk)
    for chunk in last_chunks[3:]:
        forward_sum(chunk)
    for chunk in last_chunks[:3]:
        second_sends(chunk)
    for chunk in first_chunks:
        third_sends(chunk)
    for chunk in last_chunks[3:]:
        second_sends(chunk)

    arrived("dc", dc_recv)
    sums_all = ps_sum(3)
    row = lax.broadcasted_iota(jnp.int32, (PADBITS, 128), 0)
    pbar = jnp.where(row < BITS, sums_all / TOTAL, 0.5)
    lp, lq = jnp.log(pbar), jnp.log(1.0 - pbar)
    spread = jnp.where(row < BITS, -(pbar * lp + (1.0 - pbar) * lq), 0.0)
    batch_ent = jnp.sum(spread, axis=0, keepdims=True)
    pen_out[...] = (sums_all[24:25, :] / TOTAL - batch_ent)[:, :1]
    zv = zt[...]
    smooth = jnp.tanh(zv)
    prob = jax.nn.sigmoid(2.0 * zv)
    dcodes = nt(wexp[...], ct[pl.ds(0, BLOCK), :]) + dc[:, pl.ds(0, BLOCK)] + dc_recv[...]
    fg = dcodes * (1.0 - smooth * smooth) + ENT_WEIGHT * 2.0 * prob * (1.0 - prob) * (
        -2.0 * zv - lq[:, :1] + lp[:, :1]
    )
    for i in range(BITS):
        fg_out[i] = fg[i : i + 1, :]

    for chunk in last_chunks[:3]:
        third_sends(chunk)
    for chunk in first_chunks:
        last_sum(chunk)
    for chunk in last_chunks[3:]:
        third_sends(chunk)
    for chunk in last_chunks:
        last_sum(chunk)
    for departure, size in (
        ("ag1", r3), ("ag2", r2), (("ag3", "up"), r1.at[0]), (("ag3", "dn"), r1.at[0]),
        ("tokens", ct), ("a1", prefix.at[pl.ds(0, 15)]), ("a2", prefix.at[pl.ds(0, 15)]),
        ("code", code.at[0]), (("ps", 0), ps.at[0, 0]), (("ps", 1), ps.at[1, pl.ds(0, 3)]),
        (("ps", 2), ps.at[2, pl.ds(0, 3)]), (("ps", 3), ps.at[3, pl.ds(0, 3)]), ("dc", dc_recv),
        (("rs1", 0), r1.at[0]), (("rs1", 1), r1.at[1]), ("rs2", r2), ("rs3", r3),
    ):
        departed(departure, size)
    assert (len(arrivals), len(departures)) == (ARRIVALS, DEPARTURES), (len(arrivals), len(departures))


def body(
    frames, w_query, w_key, w_value, w_out, w_code, code_bias, w_expand, w_up, w_down,
    decoder_stream, cotangent,
):
    anywhere = pl.BlockSpec(memory_space=pl.ANY)
    smem = pl.BlockSpec(memory_space=pltpu.SMEM)
    vmem = pl.BlockSpec(memory_space=pltpu.VMEM)
    scratch = [
        pltpu.VMEM((BLOCK, D), BF),
        pltpu.VMEM((D, INNER), BF),
        pltpu.VMEM((D, INNER), BF),
        pltpu.VMEM((D, INNER), BF),
        pltpu.VMEM((INNER, D), BF),
        pltpu.VMEM((2 * BLOCK, D), BF),
        pltpu.VMEM((2 * BLOCK, D), BF),
        pltpu.VMEM((4, 4, 4, 16, D), BF),
        pltpu.VMEM((4, 4, 4, 16, D), BF),
        pltpu.VMEM((BLOCK, INNER), BF),
        pltpu.VMEM((BLOCK, INNER), BF),
        pltpu.VMEM((BLOCK, INNER), BF),
        pltpu.VMEM((BLOCK, INNER), F32),
        pltpu.VMEM((INNER, HD), BF),
        pltpu.VMEM((16, SHARE, HD), BF),
        pltpu.VMEM((16, SHARE, HD), BF),
        pltpu.VMEM((INNER, HD), BF),
        pltpu.VMEM((BLOCK, D), BF),
        pltpu.VMEM((PADBITS, BLOCK), F32),
        pltpu.VMEM((2, PADBITS, BLOCK), BF),
        pltpu.VMEM((PADBITS, 2 * BLOCK), F32),
        pltpu.VMEM((PADBITS, BLOCK), F32),
        pltpu.VMEM((PADBITS, D), BF),
        pltpu.VMEM((UNITS, 2 * BLOCK), BF),
        pltpu.VMEM((UNITS, 2 * BLOCK), BF),
        pltpu.VMEM((UNITS, 256), F32),
        pltpu.VMEM((UNITS, 256), F32),
        pltpu.VMEM((UNITS, 2 * BLOCK), F32),
        pltpu.VMEM((4, 4, 4, 16, D), BF),
        pltpu.VMEM((4, 4, 4, 16, D), BF),
        pltpu.VMEM((2, 3, 3, 4, 4, 16, PART), BF),
        pltpu.VMEM((2, 3, 4, 4, 16, PART), BF),
        pltpu.VMEM((2, 3, 3, 4, 16, PART), BF),
        pltpu.VMEM((2, 3, 4, 16, PART), BF),
        pltpu.VMEM((2, 3, 3, 16, PART), BF),
        pltpu.VMEM((4, 4, PADBITS, 128), F32),
        pltpu.SemaphoreType.DMA((16,)),
        pltpu.SemaphoreType.DMA((DEPARTURES,)),
        pltpu.SemaphoreType.DMA((ARRIVALS,)),
    ]
    grads, fg, pen = pl.pallas_call(
        fused,
        out_shape=(
            jax.ShapeDtypeStruct((32, D), F32),
            jax.ShapeDtypeStruct((BITS, 1, BLOCK), F32),
            jax.ShapeDtypeStruct((1, 1), F32),
        ),
        in_specs=[anywhere] * 5 + [vmem, smem, vmem] + [anywhere] * 4,
        out_specs=(vmem,) * 3,
        scratch_shapes=scratch,
        compiler_params=pltpu.CompilerParams(
            collective_id=0, has_side_effects=True, vmem_limit_bytes=60 * 1024 * 1024
        ),
    )(
        frames.reshape(BLOCK, D), w_query, w_key, w_value, w_out, w_code.T, code_bias, w_expand,
        w_up, w_down, decoder_stream.reshape(BLOCK, D), cotangent.reshape(BLOCK, D),
    )
    return grads[:16], grads[16:], jnp.transpose(fg, (1, 2, 0)), pen[0, 0]


def solution(mesh):
    in_specs = (
        P("batch", "tm", None),
        P(),
        P(),
        P(),
        P(),
        P(),
        P(),
        P(),
        P(("tm", "batch"), None),
        P(("tm", "batch"), None),
        P("batch", "tm", None),
        P("batch", "tm", None),
    )
    out_specs = (P(("tm", "batch"), None), P(("tm", "batch"), None), P("batch", "tm", None), P())
    return jax.shard_map(body, mesh=mesh, in_specs=in_specs, out_specs=out_specs, check_vma=False)
```
